32 devices in a mesh: row: 4 (over y, x), col: 8 (over z, core).
Axes of the slice: x: 2, y: 2, z: 4, core: 2. Of those that a mesh axis runs over, the one named last changes fastest.
Arguments:
- activations: bfloat16 [512, 28672], P('col', 'row'), may hold values from -6 to 6
- act_basis: bfloat16 [28672, 28672], P('row', 'col'), may hold values from -0.03125 to 0.03125
- out_grads: bfloat16 [512, 8192], P('row', 'col'), may hold values from -0.375 to 0.375
- grad_basis: bfloat16 [8192, 8192], P('col', 'row'), may hold values from -0.0625 to 0.0625
Outputs:
- eigen_lambda: bfloat16 [8192, 28672], P('row', 'col')
The draws below stay inside these ranges and needn't reach their ends.
All inputs are finite; a program needn't handle non-finite values.
Results may differ from the reference program's by a relative error of at most 0.0058.
Values may be sent and summed in bfloat16 or wider, within the bound.
No kernel may reach another device: no remote copies, remote signals or barrier semaphores. Data moves between devices by JAX's collectives and lax.ppermute only.
A program may use at most 192 MiB of HBM per device.

```python
import jax
import jax.numpy as jnp
from jax import lax

IN = 28672
OUT = 8192
SEQS = 2
SEQ_LEN = 256
TOK = 512


def steps_of(stream_key, shape, shards, smallest, largest):
    def one(dim, parts):
        draws = jax.random.uniform(jax.random.fold_in(jax.random.fold_in(stream_key, 6), dim), (parts,), jnp.float32, smallest / len(shards), largest / len(shards))
        return jnp.repeat(jnp.exp(draws), shape[dim] // parts).reshape((-1,) + (1,) * (len(shape) - dim - 1))

    level = one(*shards[0])
    for cut in shards[1:]:
        level = level * one(*cut)
    return level


def gaussian(stream_key, extent, spread, reach, cuts=(), dtype=jnp.bfloat16):
    entries = jax.random.normal(stream_key, extent, jnp.float32) * spread
    if len(cuts) > 0:
        entries = steps_of(stream_key, extent, cuts, -0.22, 0.18) * entries
    return jnp.clip(entries, min=-reach, max=reach).astype(dtype)


def setup_inputs(seed: int = 0) -> dict:
    key_list = jax.random.split(jax.random.key(seed), 5)
    return {
        "activations": gaussian(key_list[0], (TOK, IN), 1.0, 6.0, ((0, 8), (1, 4))),
        "act_basis": gaussian(key_list[1], (IN, IN), IN ** -0.5, 0.03125, ((0, 4), (1, 8))),
        "out_grads": gaussian(key_list[2], (TOK, OUT), SEQ_LEN ** -0.5, 0.375, ((0, 4), (1, 8))),
        "grad_basis": gaussian(key_list[3], (OUT, OUT), OUT ** -0.5, 0.0625, ((0, 8), (1, 4))),
    }


def reference(activations, act_basis, out_grads, grad_basis):
    rotated_act = jnp.dot(activations, act_basis, preferred_element_type=jnp.float32).astype(jnp.bfloat16)
    rotated_grad = jnp.dot(out_grads, grad_basis, preferred_element_type=jnp.float32).astype(jnp.bfloat16)
    act_seq = rotated_act.astype(jnp.float32).reshape(SEQS, SEQ_LEN, IN)
    grad_seq = rotated_grad.astype(jnp.float32).reshape(SEQS, SEQ_LEN, OUT)
    if OUT % 512 == 0:
        block_rows = 512
    else:
        block_rows = OUT
    blocks = OUT // block_rows
    grad_blocks = jnp.moveaxis(grad_seq.reshape(SEQS, SEQ_LEN, blocks, block_rows), 2, 0)

    def one_block(grad_block):
        seq_grad = jnp.einsum("slo,sli->soi", grad_block, act_seq)
        return (jnp.sum(seq_grad * seq_grad, axis=0) / SEQS).astype(jnp.bfloat16)

    result = lax.map(one_block, grad_blocks)
    return result.reshape(OUT, IN)
```

```python
import functools

import jax
import jax.numpy as jnp
import numpy as np
from jax import lax
from jax.experimental import pallas as pl
from jax.experimental.pallas import tpu as pltpu
from jax.sharding import PartitionSpec as P

SEQS = 2
CORES = 2
F32 = jnp.float32
BF16 = jnp.bfloat16


def largest_tile(size, unit, most):
    tile = unit
    for candidate in range(unit, most + 1, unit):
        if size % candidate == 0:
            tile = candidate
    return tile if size % tile == 0 else size


def left_width(width):
    half = width // 2 // 128 * 128
    return half if half > 0 else width // 2


def chunk_dot_kernel(tile_n, split, lo_ref, hi_ref, basis_ref, *rest):
    keep_l, keep_r, send_l, send_r, total = rest
    step = pl.program_id(0)
    rows = lo_ref.shape[0]
    tokens = jnp.concatenate([lo_ref[...], hi_ref[...]], axis=0)

    @pl.when(step == 0)
    def _():
        total[...] = jnp.zeros_like(total)

    for start in range(0, total.shape[1], tile_n):
        cols = pl.ds(start, tile_n)
        total[:, cols] += jnp.dot(tokens, basis_ref[:, cols], preferred_element_type=F32)

    @pl.when(step == pl.num_programs(0) - 1)
    def _():
        left = total[:, :split]
        right = total[:, split:]
        keep_l[...] = left
        keep_r[...] = right
        send_l[...] = left.astype(BF16)
        send_r[...] = right.astype(BF16)


def chunk_dot(lo, hi, basis):
    rows, depth = lo.shape
    width = basis.shape[1]
    split = left_width(width)
    tile_k = largest_tile(depth, 256, 512)
    tile_n = largest_tile(width, 128, 512)
    tokens = 2 * rows
    shapes = [(tokens, split), (tokens, width - split)]
    return pl.pallas_call(
        functools.partial(chunk_dot_kernel, tile_n, split),
        grid=(depth // tile_k,),
        in_specs=[
            pl.BlockSpec((rows, tile_k), lambda k: (0, k)),
            pl.BlockSpec((rows, tile_k), lambda k: (0, k)),
            pl.BlockSpec((tile_k, width), lambda k: (k, 0)),
        ],
        out_specs=[pl.BlockSpec(s, lambda k: (0, 0)) for s in shapes + shapes],
        out_shape=[jax.ShapeDtypeStruct(s, F32) for s in shapes]
        + [jax.ShapeDtypeStruct(s, BF16) for s in shapes],
        scratch_shapes=[pltpu.VMEM((tokens, width), F32)],
        compiler_params=pltpu.CompilerParams(vmem_limit_bytes=32 * 2**20),
        cost_estimate=pl.CostEstimate(
            flops=2 * tokens * depth * width,
            bytes_accessed=2 * depth * width,
            transcendentals=0,
        ),
        name="chunk_dot",
    )(lo, hi, basis)


def lambda_kernel(chunks, split, tile_n, place_ref, own_ref, sib_ref, *rest):
    parts, out_ref, acts = rest[: 2 * chunks], rest[-2], rest[-1]
    tokens = parts[0].shape[0] // CORES

    @pl.when(pl.program_id(0) == 0)
    def _():
        for c in range(chunks):
            for h in range(CORES):
                at = pl.multiple_of(place_ref[CORES * c + h] * tokens, tokens)
                rows = pl.ds(at, tokens)
                here = pl.ds(h * tokens, tokens)
                acts[rows, :split] = parts[2 * c][here, :]
                acts[rows, split:] = parts[2 * c + 1][here, :]

    half = acts.shape[0] // 2
    for start in range(0, acts.shape[1], tile_n):
        cols = pl.ds(start, tile_n)
        first = jnp.dot(own_ref[...], acts[:half, cols], preferred_element_type=F32)
        second = jnp.dot(sib_ref[...], acts[half:, cols], preferred_element_type=F32)
        out_ref[:, cols] = ((first * first + second * second) * (1.0 / SEQS)).astype(BF16)


def lambda_product(place, own, sib, parts):
    out_rows, seq_tokens = own.shape
    chunks = len(parts) // 2
    split = parts[0].shape[1]
    width = split + parts[1].shape[1]
    tile_o = largest_tile(out_rows, 128, 256)
    tile_n = largest_tile(width, 128, 512)
    whole = lambda o, place: (0, 0)
    return pl.pallas_call(
        functools.partial(lambda_kernel, chunks, split, tile_n),
        grid_spec=pltpu.PrefetchScalarGridSpec(
            num_scalar_prefetch=1,
            grid=(out_rows // tile_o,),
            in_specs=[
                pl.BlockSpec((tile_o, seq_tokens), lambda o, place: (o, 0)),
                pl.BlockSpec((tile_o, seq_tokens), lambda o, place: (o, 0)),
            ]
            + [pl.BlockSpec(p.shape, whole) for p in parts],
            out_specs=pl.BlockSpec((tile_o, width), lambda o, place: (o, 0)),
            scratch_shapes=[pltpu.VMEM((SEQS * seq_tokens, width), BF16)],
        ),
        out_shape=jax.ShapeDtypeStruct((out_rows, width), BF16),
        compiler_params=pltpu.CompilerParams(vmem_limit_bytes=32 * 2**20),
        cost_estimate=pl.CostEstimate(
            flops=2 * out_rows * width * SEQS * seq_tokens,
            bytes_accessed=2 * out_rows * width,
            transcendentals=0,
        ),
        name="lambda_product",
    )(place, own, sib, *parts)


def chip_ring(chips):
    order = list(range(1, chips, 2))
    order = [0] + order + [c for c in range(chips - 1, 0, -1) if c % 2 == 0]
    return {order[i]: order[(i + 1) % chips] for i in range(chips)}


def on_both_cores(pairs):
    return [(CORES * a + k, CORES * b + k) for a, b in pairs for k in range(CORES)]


def local(rows_n, cols_n, activations, act_basis, out_grads, grad_basis):
    chips = cols_n // CORES
    col = lax.axis_index("col")
    core = col & 1
    sibling = [(c, c ^ 1) for c in range(cols_n)]
    swap = lambda x: lax.ppermute(x, "col", sibling)
    bits = [1 << b for b in range(rows_n.bit_length() - 1)]
    trade = lambda x, bit: lax.ppermute(x, "row", [(r, r ^ bit) for r in range(rows_n)])

    succ = chip_ring(chips)
    pred = {b: a for a, b in succ.items()}
    ring = on_both_cores(sorted(succ.items()))
    blocks = [activations]
    for _ in range(chips - 1):
        blocks.append(lax.ppermute(blocks[-1], "col", ring))
    sib_blocks = [swap(b) for b in blocks]

    grads = out_grads
    row = lax.axis_index("row")
    for bit in bits:
        other = trade(grads, bit)
        upper = (row & bit) != 0
        grads = jnp.where(
            upper,
            jnp.concatenate([other, grads], axis=0),
            jnp.concatenate([grads, other], axis=0),
        )
    part = lax.dot_general(
        grad_basis, grads, (((0,), (1,)), ((), ())), preferred_element_type=F32
    )
    seq_tokens = part.shape[1] // SEQS
    seqs = [part[:, :seq_tokens], part[:, seq_tokens:]]
    mine = jnp.where(core == 0, seqs[0], seqs[1])
    theirs = jnp.where(core == 0, seqs[1], seqs[0]).astype(BF16)
    mine = mine + swap(theirs).astype(F32)
    pieces = []
    piece_rows = mine.shape[0] // 2
    for p in range(2):
        total = mine[p * piece_rows : (p + 1) * piece_rows]
        for j in range(chips // 2 - 1):
            inward = [(j, j + 1), (chips - 1 - j, chips - 2 - j)]
            total = total + lax.ppermute(
                total.astype(BF16), "col", on_both_cores(inward)
            ).astype(F32)
        mid = chips // 2
        total = total + lax.ppermute(
            total.astype(BF16), "col", on_both_cores([(mid - 1, mid), (mid, mid - 1)])
        ).astype(F32)
        final = total.astype(BF16)
        for j in range(mid - 1, 0, -1):
            got = lax.ppermute(
                final, "col", on_both_cores([(j, j - 1), (chips - 1 - j, chips - j)])
            )
            takes = jnp.asarray([c // CORES in (j - 1, chips - j) for c in range(cols_n)])
            final = jnp.where(takes[col], got, final)
        pieces.append(final)
    own = jnp.concatenate(pieces, axis=0)
    sib = swap(own)

    parts = []
    for lo, hi in zip(blocks, sib_blocks):
        keep_l, keep_r, send_l, send_r = chunk_dot(lo, hi, act_basis)
        for i in range(len(bits)):
            got_l = trade(send_l, bits[i])
            got_r = trade(send_r, bits[-1 - i])
            keep_l = keep_l + got_l.astype(F32)
            keep_r = keep_r + got_r.astype(F32)
            send_l, send_r = keep_l.astype(BF16), keep_r.astype(BF16)
        parts += [send_l, send_r]
    place = np.zeros((cols_n, CORES * chips), np.int32)
    for c in range(cols_n):
        here, k = c // CORES, c % CORES
        for s in range(chips):
            block = (here + k * (chips // SEQS)) % chips
            place[c, CORES * s : CORES * (s + 1)] = CORES * block + k, CORES * block + 1 - k
            here = pred[here]
    place = lax.dynamic_index_in_dim(jnp.asarray(place), col, 0, keepdims=False)
    return lambda_product(place, own, sib, parts)


def solution(mesh):
    rows_n, cols_n = mesh.shape["row"], mesh.shape["col"]

    def body(activations, act_basis, out_grads, grad_basis):
        return local(rows_n, cols_n, activations, act_basis, out_grads, grad_basis)

    return jax.shard_map(
        body,
        mesh=mesh,
        in_specs=(P("col", "row"), P("row", "col"), P("row", "col"), P("col", "row")),
        out_specs=P("row", "col"),
        check_vma=False,
    )
```

```python
import functools

import jax
import jax.numpy as jnp
import numpy as np
from jax import lax
from jax.experimental import pallas as pl
from jax.experimental.pallas import tpu as pltpu
from jax.sharding import PartitionSpec as P

SEQS = 2
CORES = 2
F32 = jnp.float32
BF16 = jnp.bfloat16
ANYWHERE = pl.BlockSpec(memory_space=pl.ANY)


def largest_tile(size, unit, most):
    tile = unit
    for candidate in range(unit, most + 1, unit):
        if size % candidate == 0:
            tile = candidate
    return tile if size % tile == 0 else size


def column_parts(width):
    if width % 256:
        return [(0, width)]
    return [(0, width // 2), (width // 2, width // 2)]


def column_tile(start, width):
    for tile in (256, 128):
        if start % tile == 0 and width % tile == 0:
            return tile
    raise ValueError("columns")


def gate(x, after):
    return pl.pallas_call(
        lambda x_ref, after_ref, out_ref: None,
        in_specs=[ANYWHERE, ANYWHERE],
        out_specs=ANYWHERE,
        out_shape=jax.ShapeDtypeStruct(x.shape, x.dtype),
        input_output_aliases={0: 0},
        cost_estimate=pl.CostEstimate(flops=0, bytes_accessed=0, transcendentals=0),
        name="gate",
    )(x, after)


def chunk_dot_kernel(count, upper_ref, *rest):
    blocks, basis_ref, keep_ref, send_ref = rest[:count], rest[count], rest[-2], rest[-1]
    tokens = jnp.concatenate([b[...] for b in blocks], axis=0)
    total = jnp.dot(tokens, basis_ref[...], preferred_element_type=F32)
    half = total.shape[0] // 2
    upper = upper_ref[0] != 0
    keep_ref[...] = jnp.where(upper, total[half:], total[:half])
    send_ref[...] = jnp.where(upper, total[:half], total[half:]).astype(BF16)


def chunk_dot(upper, blocks, basis, start, width, after=()):
    rows, depth = blocks[0].shape
    tokens = rows * len(blocks)
    tile = column_tile(start, width)
    first = start // tile
    count = len(blocks)

    def kernel(upper_ref, *rest):
        chunk_dot_kernel(count, upper_ref, *rest[: count + 1], *rest[-2:])

    shape = (tokens // 2, width)
    return pl.pallas_call(
        kernel,
        grid_spec=pltpu.PrefetchScalarGridSpec(
            num_scalar_prefetch=1,
            grid=(width // tile,),
            in_specs=[pl.BlockSpec((rows, depth), lambda n, s: (0, 0))] * count
            + [pl.BlockSpec((depth, tile), lambda n, s: (0, first + n))]
            + [ANYWHERE] * len(after),
            out_specs=[pl.BlockSpec((tokens // 2, tile), lambda n, s: (0, n))] * 2,
        ),
        out_shape=[jax.ShapeDtypeStruct(shape, F32), jax.ShapeDtypeStruct(shape, BF16)],
        compiler_params=pltpu.CompilerParams(vmem_limit_bytes=40 * 2**20),
        cost_estimate=pl.CostEstimate(
            flops=2 * tokens * depth * width,
            bytes_accessed=2 * depth * width,
            transcendentals=0,
        ),
        name="chunk_dot",
    )(upper, *blocks, basis, *after)


def lambda_kernel(count, unit, place_ref, own_ref, sib_ref, *rest):
    parts, out_ref, acts = rest[:count], rest[-2], rest[-1]

    @pl.when(pl.program_id(0) == 0)
    def _():
        at = 0
        for part in parts:
            for h in range(part.shape[0] // unit):
                rows = pl.ds(pl.multiple_of(place_ref[at] * unit, unit), unit)
                acts[rows, :] = part[h * unit : (h + 1) * unit, :]
                at += 1

    half = acts.shape[0] // 2
    tile = largest_tile(acts.shape[1], 128, 512)
    for start in range(0, acts.shape[1], tile):
        cols = pl.ds(start, tile)
        first = jnp.dot(own_ref[...], acts[:half, cols], preferred_element_type=F32)
        second = jnp.dot(sib_ref[...], acts[half:, cols], preferred_element_type=F32)
        out_ref[:, cols] = ((first * first + second * second) * (1.0 / SEQS)).astype(BF16)


def lambda_product(place, own, sib, parts, unit, start, width, so_far):
    out_rows, seq_tokens = own.shape
    tile_o = largest_tile(out_rows, 128, 256)
    whole = lambda o, place: (0, 0)
    at = start // width
    total_width = so_far[1]
    given = [] if so_far[0] is None else [so_far[0]]
    count = len(parts)

    def kernel(place_ref, own_ref, sib_ref, *rest):
        lambda_kernel(count, unit, place_ref, own_ref, sib_ref, *rest[:count], *rest[-2:])

    return pl.pallas_call(
        kernel,
        grid_spec=pltpu.PrefetchScalarGridSpec(
            num_scalar_prefetch=1,
            grid=(out_rows // tile_o,),
            in_specs=[
                pl.BlockSpec((tile_o, seq_tokens), lambda o, place: (o, 0)),
                pl.BlockSpec((tile_o, seq_tokens), lambda o, place: (o, 0)),
            ]
            + [pl.BlockSpec(p.shape, whole) for p in parts]
            + [ANYWHERE] * len(given),
            out_specs=pl.BlockSpec((tile_o, width), lambda o, place: (o, at)),
            scratch_shapes=[pltpu.VMEM((SEQS * seq_tokens, width), BF16)],
        ),
        out_shape=jax.ShapeDtypeStruct((out_rows, total_width), BF16),
        input_output_aliases={3 + count: 0} if given else {},
        compiler_params=pltpu.CompilerParams(vmem_limit_bytes=40 * 2**20),
        cost_estimate=pl.CostEstimate(
            flops=2 * out_rows * width * SEQS * seq_tokens,
            bytes_accessed=2 * out_rows * width,
            transcendentals=0,
        ),
        name="lambda_product",
    )(place, own, sib, *parts, *given)


def chip_ring(chips):
    order = list(range(1, chips, 2))
    order = [0] + order + [c for c in range(chips - 1, 0, -1) if c % 2 == 0]
    return {order[i]: order[(i + 1) % chips] for i in range(chips)}


def on_both_cores(pairs):
    return [(CORES * a + k, CORES * b + k) for a, b in pairs for k in range(CORES)]


def powers(n):
    return [1 << b for b in range(n.bit_length() - 1)]


def halves(x, upper):
    half = x.shape[0] // 2
    low, high = x[:half], x[half:]
    return jnp.where(upper, high, low), jnp.where(upper, low, high)


def joined(mine, theirs, upper):
    return jnp.where(
        upper,
        jnp.concatenate([theirs, mine], axis=0),
        jnp.concatenate([mine, theirs], axis=0),
    )


def token_chunks(chips):
    chunks = [[0]]
    if chips > 2:
        chunks.append(list(range(1, chips - 1)))
    if chips > 1:
        chunks.append([chips - 1])
    return chunks


def local(rows_n, cols_n, activations, act_basis, out_grads, grad_basis):
    chips = cols_n // CORES
    col = lax.axis_index("col")
    row = lax.axis_index("row")
    core = col & 1
    swap = lambda x: lax.ppermute(x, "col", [(c, c ^ 1) for c in range(cols_n)])
    trade = lambda x, bit: lax.ppermute(x, "row", [(r, r ^ bit) for r in range(rows_n)])
    bits = powers(rows_n)
    rank_bit = [jnp.reshape((row & b).astype(jnp.int32), (1,)) for b in bits]

    succ = chip_ring(chips)
    pred = {b: a for a, b in succ.items()}
    ring = on_both_cores(sorted(succ.items()))
    blocks = [activations]
    for _ in range(chips - 1):
        blocks.append(lax.ppermute(blocks[-1], "col", ring))
    pairs = [(b, swap(b)) for b in blocks]

    grads = gate(out_grads, pairs[0][1])
    for bit in bits:
        grads = joined(grads, trade(grads, bit), (row & bit) != 0)
    part = lax.dot_general(
        grad_basis, grads, (((0,), (1,)), ((), ())), preferred_element_type=F32
    )
    seq_tokens = part.shape[1] // SEQS
    seqs = [part[:, :seq_tokens], part[:, seq_tokens:]]
    mine = jnp.where(core == 0, seqs[0], seqs[1])
    theirs = jnp.where(core == 0, seqs[1], seqs[0]).astype(BF16)
    mine = mine + swap(theirs).astype(F32)
    steps = powers(chips)
    late = blocks[max(chips - 2, 0)]
    for bit in steps:
        mine, away = halves(mine, (col & (CORES * bit)) != 0)
        away = away.astype(BF16)
        if bit == 1:
            away = gate(away, late)
        step = on_both_cores([(c, c ^ bit) for c in range(chips)])
        mine = mine + lax.ppermute(away, "col", step).astype(F32)
    own = mine.astype(BF16)
    for bit in reversed(steps):
        step = on_both_cores([(c, c ^ bit) for c in range(chips)])
        own = joined(own, lax.ppermute(own, "col", step), (col & (CORES * bit)) != 0)
    sib = swap(own)

    width = act_basis.shape[1]
    ranges = column_parts(width)
    orders = [bits, bits[::-1]]
    results = [[] for _ in ranges]
    before = ()
    for chunk in token_chunks(chips):
        tokens = [b for s in chunk for b in pairs[s]]
        for side, (start, wide) in enumerate(ranges):
            order = orders[side]
            first = bits.index(order[0])
            keep, send = chunk_dot(rank_bit[first], tokens, act_basis, start, wide, before)
            before = (send,)
            keep = keep + trade(send, order[0]).astype(F32)
            for bit in order[1:]:
                keep = keep + trade(keep.astype(BF16), bit).astype(F32)
            mine = keep.astype(BF16)
            results[side] += [mine, trade(mine, order[0])]

    unit = activations.shape[0]
    out, done_width = None, width
    for side, (start, wide) in enumerate(ranges):
        table = np.zeros((rows_n, cols_n, CORES * chips), np.int32)
        for r in range(rows_n):
            for c in range(cols_n):
                here, k = c // CORES, c % CORES
                place = []
                for s in range(chips):
                    block = (here + k * (chips // SEQS)) % chips
                    place.append([CORES * block + k, CORES * block + 1 - k])
                    here = pred[here]
                flat = []
                for chunk in token_chunks(chips):
                    units = [u for s in chunk for u in place[s]]
                    n = len(units) // 2
                    low, high = units[:n], units[n:]
                    flat += high + low if r & orders[side][0] else low + high
                table[r, c] = flat
        where = jnp.asarray(table.reshape(rows_n * cols_n, -1))
        where = lax.dynamic_index_in_dim(where, row * cols_n + col, 0, keepdims=False)
        out = lambda_product(
            where, own, sib, results[side], unit, start, wide, (out, done_width)
        )
    return out


def solution(mesh):
    rows_n, cols_n = mesh.shape["row"], mesh.shape["col"]

    def body(activations, act_basis, out_grads, grad_basis):
        return local(rows_n, cols_n, activations, act_basis, out_grads, grad_basis)

    return jax.shard_map(
        body,
        mesh=mesh,
        in_specs=(P("col", "row"), P("row", "col"), P("row", "col"), P("col", "row")),
        out_specs=P("row", "col"),
        check_vma=False,
    )
```

```python
import functools

import jax
import jax.numpy as jnp
import numpy as np
from jax import lax
from jax.experimental import pallas as pl
from jax.experimental.pallas import tpu as pltpu
from jax.sharding import PartitionSpec as P

SEQS = 2
CORES = 2
F32 = jnp.float32
BF16 = jnp.bfloat16
ANYWHERE = pl.BlockSpec(memory_space=pl.ANY)


def largest_tile(size, unit, most):
    tile = unit
    for candidate in range(unit, most + 1, unit):
        if size % candidate == 0:
            tile = candidate
    return tile if size % tile == 0 else size


def column_parts(width):
    small = width // 7
    if width % 7 or small % 128:
        return [(0, width)]
    return [(0, 3 * small), (3 * small, 3 * small), (6 * small, small)]


def column_tile(start, width):
    for tile in (256, 128):
        if start % tile == 0 and width % tile == 0:
            return tile
    raise ValueError("columns")


NO_COST = pl.CostEstimate(flops=0, bytes_accessed=0, transcendentals=0)


def gate(x, *after):
    return pl.pallas_call(
        lambda *refs: None,
        in_specs=[ANYWHERE] * (1 + len(after)),
        out_specs=ANYWHERE,
        out_shape=jax.ShapeDtypeStruct(x.shape, x.dtype),
        input_output_aliases={0: 0},
        cost_estimate=NO_COST,
        name="gate",
    )(x, *after)


def copy_gate(x, after):
    def kernel(x_ref, after_ref, out_ref):
        out_ref[...] = x_ref[...]

    return pl.pallas_call(
        kernel,
        in_specs=[pl.BlockSpec(memory_space=pltpu.VMEM), ANYWHERE],
        out_specs=pl.BlockSpec(memory_space=pltpu.VMEM),
        out_shape=jax.ShapeDtypeStruct(x.shape, x.dtype),
        cost_estimate=NO_COST,
        name="copy_gate",
    )(x, after)


def chunk_dot(upper, blocks, basis, start, width, after=()):
    rows, depth = blocks[0].shape
    tokens = rows * len(blocks)
    tile = column_tile(start, width)
    first = start // tile
    count = len(blocks)
    cuts = 4 if depth % 1024 == 0 else 1
    deep = depth // cuts

    def kernel(upper_ref, *rest):
        block_refs, basis_refs = rest[:count], rest[count : count + cuts]
        keep_ref, send_ref = rest[-2:]
        total = None
        for i, basis_ref in enumerate(basis_refs):
            ks = slice(i * deep, (i + 1) * deep)
            piece = jnp.concatenate([b[:, ks] for b in block_refs], axis=0)
            term = jnp.dot(piece, basis_ref[...], preferred_element_type=F32)
            total = term if total is None else total + term
        half = tokens // 2
        is_upper = upper_ref[0] != 0
        keep_ref[...] = jnp.where(is_upper, total[half:], total[:half])
        send_ref[...] = jnp.where(is_upper, total[:half], total[half:]).astype(BF16)

    def column_block(i):
        return pl.BlockSpec((deep, tile), lambda n, s: (i, first + n))

    shape = (tokens // 2, width)
    return pl.pallas_call(
        kernel,
        grid_spec=pltpu.PrefetchScalarGridSpec(
            num_scalar_prefetch=1,
            grid=(width // tile,),
            in_specs=[pl.BlockSpec((rows, depth), lambda n, s: (0, 0))] * count
            + [column_block(i) for i in range(cuts)]
            + [ANYWHERE] * len(after),
            out_specs=[pl.BlockSpec((tokens // 2, tile), lambda n, s: (0, n))] * 2,
        ),
        out_shape=[jax.ShapeDtypeStruct(shape, F32), jax.ShapeDtypeStruct(shape, BF16)],
        compiler_params=pltpu.CompilerParams(vmem_limit_bytes=40 * 2**20),
        cost_estimate=pl.CostEstimate(
            flops=tokens * depth * width // 8,
            bytes_accessed=depth * width // 8,
            transcendentals=0,
        ),
        name="chunk_dot",
    )(upper, *blocks, *[basis] * cuts, *after)


def lambda_kernel(count, unit, place_ref, own_ref, sib_ref, *rest):
    parts, out_ref, acts = rest[:count], rest[-2], rest[-1]

    @pl.when(pl.program_id(0) == 0)
    def _():
        at = 0
        for part in parts:
            for h in range(part.shape[0] // unit):
                rows = pl.ds(pl.multiple_of(place_ref[at] * unit, unit), unit)
                acts[rows, :] = part[h * unit : (h + 1) * unit, :]
                at += 1

    half = acts.shape[0] // 2
    tile = largest_tile(acts.shape[1], 128, 512)
    for start in range(0, acts.shape[1], tile):
        cols = pl.ds(start, tile)
        first = jnp.dot(own_ref[...], acts[:half, cols], preferred_element_type=F32)
        second = jnp.dot(sib_ref[...], acts[half:, cols], preferred_element_type=F32)
        out_ref[:, cols] = ((first * first + second * second) * (1.0 / SEQS)).astype(BF16)


def lambda_product(place, own, sib, parts, unit, start, width, so_far):
    out_rows, seq_tokens = own.shape
    tile_o = largest_tile(out_rows, 128, 512)
    whole = lambda o, place: (0, 0)
    at = start // width
    total_width = so_far[1]
    given = [] if so_far[0] is None else [so_far[0]]
    count = len(parts)

    def kernel(place_ref, own_ref, sib_ref, *rest):
        lambda_kernel(count, unit, place_ref, own_ref, sib_ref, *rest[:count], *rest[-2:])

    return pl.pallas_call(
        kernel,
        grid_spec=pltpu.PrefetchScalarGridSpec(
            num_scalar_prefetch=1,
            grid=(out_rows // tile_o,),
            in_specs=[
                pl.BlockSpec((tile_o, seq_tokens), lambda o, place: (o, 0)),
                pl.BlockSpec((tile_o, seq_tokens), lambda o, place: (o, 0)),
            ]
            + [pl.BlockSpec(p.shape, whole) for p in parts]
            + [ANYWHERE] * len(given),
            out_specs=pl.BlockSpec((tile_o, width), lambda o, place: (o, at)),
            scratch_shapes=[pltpu.VMEM((SEQS * seq_tokens, width), BF16)],
        ),
        out_shape=jax.ShapeDtypeStruct((out_rows, total_width), BF16),
        input_output_aliases={3 + count: 0} if given else {},
        compiler_params=pltpu.CompilerParams(vmem_limit_bytes=40 * 2**20),
        cost_estimate=pl.CostEstimate(
            flops=2 * out_rows * width * SEQS * seq_tokens,
            bytes_accessed=2 * out_rows * width,
            transcendentals=0,
        ),
        name="lambda_product",
    )(place, own, sib, *parts, *given)


def chip_ring(chips):
    order = list(range(1, chips, 2))
    order = [0] + order + [c for c in range(chips - 1, 0, -1) if c % 2 == 0]
    return {order[i]: order[(i + 1) % chips] for i in range(chips)}


def on_both_cores(pairs):
    return [(CORES * a + k, CORES * b + k) for a, b in pairs for k in range(CORES)]


def powers(n):
    return [1 << b for b in range(n.bit_length() - 1)]


def halves(x, upper):
    half = x.shape[0] // 2
    low, high = x[:half], x[half:]
    return jnp.where(upper, high, low), jnp.where(upper, low, high)


def joined(mine, theirs, upper):
    return jnp.where(
        upper,
        jnp.concatenate([theirs, mine], axis=0),
        jnp.concatenate([mine, theirs], axis=0),
    )


def token_chunks(chips):
    half = max(chips // 2, 1)
    return [c for c in (list(range(half)), list(range(half, chips))) if c]


def local(rows_n, cols_n, activations, act_basis, out_grads, grad_basis):
    chips = cols_n // CORES
    col = lax.axis_index("col")
    row = lax.axis_index("row")
    core = col & 1
    swap = lambda x: lax.ppermute(x, "col", [(c, c ^ 1) for c in range(cols_n)])
    trade = lambda x, bit: lax.ppermute(x, "row", [(r, r ^ bit) for r in range(rows_n)])
    bits = powers(rows_n)
    rank_bit = [jnp.reshape((row & b).astype(jnp.int32), (1,)) for b in bits]

    succ = chip_ring(chips)
    pred = {b: a for a, b in succ.items()}
    ring = on_both_cores(sorted(succ.items()))
    blocks = [activations]
    for _ in range(chips - 1):
        blocks.append(lax.ppermute(blocks[-1], "col", ring))
    pairs = [(b, swap(b)) for b in blocks]

    grads = copy_gate(out_grads, pairs[0][1])
    for bit in bits:
        grads = joined(grads, trade(grads, bit), (row & bit) != 0)
    grads = gate(grads, blocks[min(1, chips - 1)])
    part = lax.dot_general(
        grad_basis, grads, (((0,), (1,)), ((), ())), preferred_element_type=F32
    )
    seq_tokens = part.shape[1] // SEQS
    seqs = [part[:, :seq_tokens], part[:, seq_tokens:]]
    mine = jnp.where(core == 0, seqs[0], seqs[1])
    theirs = jnp.where(core == 0, seqs[1], seqs[0]).astype(BF16)
    mine = mine + swap(theirs).astype(F32)
    chip_bits = powers(chips)
    chip_trade = lambda x, bit: lax.ppermute(
        x, "col", on_both_cores([(c, c ^ bit) for c in range(chips)])
    )
    upper_chip = (col & CORES) != 0

    width = act_basis.shape[1]
    ranges = column_parts(width)
    orders = [bits, bits[::-1], bits][: len(ranges)]
    chunks = token_chunks(chips)
    tasks = []
    for n in range(len(chunks)):
        sides = list(range(len(ranges)))
        tasks += [(n, s) for s in (sides if n else sides[:1] + sides[:0:-1])]
    results = [[] for _ in ranges]
    halved, summed, before = [], [], []
    for at, (n, side) in enumerate(tasks):
        tokens = [b for s in chunks[n] for b in pairs[s]]
        start, wide = ranges[side]
        order = orders[side]
        if n == 0 and at == len(ranges) - 1:
            before.append(blocks[chips // 2])
        if n == 1 and side == 0:
            mine, away = halves(mine, upper_chip)
            away = gate(away.astype(BF16), blocks[-1])
            before.append(away)
            mine = mine + chip_trade(away, 1).astype(F32)
        keep, send = chunk_dot(
            rank_bit[bits.index(order[0])], tokens, act_basis, start, wide, before
        )
        before = [send]
        if n == 1 and side == 0:
            for bit in chip_bits[1:]:
                away = mine.astype(BF16)
                if bit == chip_bits[1]:
                    away = gate(away, send)
                    before.append(away)
                mine = mine + chip_trade(away, bit).astype(F32)
        for keep_s, order_s, side_s in summed:
            done = gate(keep_s.astype(BF16), send)
            before.append(done)
            results[side_s] += [done, trade(done, order_s[0])]
        summed = []
        for keep_h, order_h, side_h in halved:
            for bit in order_h[1:]:
                away = keep_h.astype(BF16)
                if bit == order_h[1]:
                    away = gate(away, send)
                    before.append(away)
                keep_h = keep_h + trade(away, bit).astype(F32)
            summed.append((keep_h, order_h, side_h))
        halved = [(keep + trade(send, order[0]).astype(F32), order, side)]
    for keep_h, order_h, side_h in halved:
        for bit in order_h[1:]:
            keep_h = keep_h + trade(keep_h.astype(BF16), bit).astype(F32)
        summed.append((keep_h, order_h, side_h))
    for keep_s, order_s, side_s in summed:
        done = keep_s.astype(BF16)
        results[side_s] += [done, trade(done, order_s[0])]
    own = gate(mine.astype(BF16), send)
    own = joined(own, gate(chip_trade(own, 1), done), upper_chip)
    sib = swap(own)

    unit = activations.shape[0]
    out, done_width = None, width
    for side, (start, wide) in enumerate(ranges):
        table = np.zeros((rows_n, cols_n, CORES * chips), np.int32)
        for r in range(rows_n):
            for c in range(cols_n):
                here, k = c // CORES, c % CORES
                place = []
                for s in range(chips):
                    block = (here + k * (chips // SEQS)) % chips
                    place.append([CORES * block + k, CORES * block + 1 - k])
                    here = pred[here]
                flat = []
                for chunk in chunks:
                    units = [u for s in chunk for u in place[s]]
                    n = len(units) // 2
                    low, high = units[:n], units[n:]
                    flat += high + low if r & orders[side][0] else low + high
                table[r, c] = flat
        where = jnp.asarray(table.reshape(rows_n * cols_n, -1))
        where = lax.dynamic_index_in_dim(where, row * cols_n + col, 0, keepdims=False)
        out = lambda_product(
            where, own, sib, results[side], unit, start, wide, (out, done_width)
        )
    return out


def solution(mesh):
    rows_n, cols_n = mesh.shape["row"], mesh.shape["col"]

    def body(activations, act_basis, out_grads, grad_basis):
        return local(rows_n, cols_n, activations, act_basis, out_grads, grad_basis)

    return jax.shard_map(
        body,
        mesh=mesh,
        in_specs=(P("col", "row"), P("row", "col"), P("row", "col"), P("col", "row")),
        out_specs=P("row", "col"),
        check_vma=False,
    )
```

```python
import functools

import jax
import jax.numpy as jnp
import numpy as np
from jax import lax
from jax.experimental import pallas as pl
from jax.experimental.pallas import tpu as pltpu
from jax.sharding import PartitionSpec as P

SEQS = 2
CORES = 2
F32 = jnp.float32
BF16 = jnp.bfloat16
ANYWHERE = pl.BlockSpec(memory_space=pl.ANY)
IN_VMEM = pl.BlockSpec(memory_space=pltpu.VMEM)


def vmem(mib):
    return pltpu.CompilerParams(vmem_limit_bytes=mib * 2**20)


def largest_tile(size, unit, most):
    tile = unit
    for candidate in range(unit, most + 1, unit):
        if size % candidate == 0:
            tile = candidate
    return tile if size % tile == 0 else size


def column_parts(width, pieces):
    unit = width // 7
    if width % 7 or unit % 128:
        return [(0, width)]
    sevenths = {2: [4, 3], 3: [3, 2, 2]}[pieces]
    return [(unit * sum(sevenths[:i]), unit * n) for i, n in enumerate(sevenths)]


def column_tile(start, width):
    for tile in (512, 256, 128):
        if start % tile == 0 and width % tile == 0:
            return tile
    raise ValueError("columns")


NO_COST = pl.CostEstimate(flops=0, bytes_accessed=0, transcendentals=0)


def gate(x, *after):
    return pl.pallas_call(
        lambda *refs: None,
        in_specs=[ANYWHERE] * (1 + len(after)),
        out_specs=ANYWHERE,
        out_shape=jax.ShapeDtypeStruct(x.shape, x.dtype),
        input_output_aliases={0: 0},
        compiler_params=vmem(1),
        cost_estimate=NO_COST,
        name="gate",
    )(x, *after)


def copy_gate(x, after):
    def kernel(x_ref, after_ref, out_ref):
        out_ref[...] = x_ref[...]

    return pl.pallas_call(
        kernel,
        in_specs=[pl.BlockSpec(memory_space=pltpu.VMEM), ANYWHERE],
        out_specs=pl.BlockSpec(memory_space=pltpu.VMEM),
        out_shape=jax.ShapeDtypeStruct(x.shape, x.dtype),
        compiler_params=vmem(2),
        cost_estimate=NO_COST,
        name="copy_gate",
    )(x, after)


def chunk_dot(upper, blocks, basis, start, width, after=()):
    rows, depth = blocks[0].shape
    tokens = rows * len(blocks)
    tile = column_tile(start, width)
    first = start // tile
    count = len(blocks)
    deep = largest_tile(depth, 256, 1792)
    steps = depth // deep

    def kernel(upper_ref, *rest):
        block_refs, basis_ref = rest[:count], rest[count]
        keep_ref, send_ref, total = rest[-3:]
        k = pl.program_id(1)
        ks = pl.ds(pl.multiple_of(k * deep, deep), deep)
        piece = jnp.concatenate([b[:, ks] for b in block_refs], axis=0)
        term = jnp.dot(piece, basis_ref[...], preferred_element_type=F32)

        @pl.when(k == 0)
        def _():
            total[...] = term

        @pl.when(jnp.logical_and(k > 0, k < steps - 1))
        def _():
            total[...] += term

        @pl.when(k == steps - 1)
        def _():
            whole = (total[...] + term).astype(BF16)
            half = tokens // 2
            is_upper = upper_ref[0] != 0
            keep_ref[...] = jnp.where(is_upper, whole[half:], whole[:half])
            send_ref[...] = jnp.where(is_upper, whole[:half], whole[half:])

    shape = (tokens // 2, width)
    return pl.pallas_call(
        kernel,
        grid_spec=pltpu.PrefetchScalarGridSpec(
            num_scalar_prefetch=1,
            grid=(width // tile, steps),
            in_specs=[IN_VMEM] * count
            + [pl.BlockSpec((deep, tile), lambda n, k, s: (k, first + n))]
            + [ANYWHERE] * len(after),
            out_specs=[pl.BlockSpec((tokens // 2, tile), lambda n, k, s: (0, n))] * 2,
            scratch_shapes=[pltpu.VMEM((tokens, tile), F32)],
        ),
        out_shape=[jax.ShapeDtypeStruct(shape, BF16)] * 2,
        compiler_params=vmem(20),
        cost_estimate=pl.CostEstimate(
            flops=tokens * depth * width // 8,
            bytes_accessed=depth * width // 8,
            transcendentals=0,
        ),
        name="chunk_dot",
    )(upper, *blocks, basis, *after)


def lambda_product(place, own, sib, parts, unit, width):
    out_rows, seq_tokens = own.shape
    tile_o = largest_tile(out_rows, 128, 256)
    tile_n = largest_tile(width, 128, 512)
    starts = [start for start, _ in parts]
    arrays = [array for _, array in parts]
    count = len(arrays)

    def kernel(place_ref, own_ref, sib_ref, *rest):
        part_refs, out_ref, acts = rest[:count], rest[-2], rest[-1]

        @pl.when(pl.program_id(0) == 0)
        def _():
            at = 0
            for start, part in zip(starts, part_refs):
                cols = slice(start, start + part.shape[1])
                for h in range(part.shape[0] // unit):
                    rows = pl.ds(pl.multiple_of(place_ref[at] * unit, unit), unit)
                    acts[rows, cols] = part[h * unit : (h + 1) * unit, :]
                    at += 1

        half = acts.shape[0] // 2
        for start in range(0, width, tile_n):
            cols = pl.ds(start, tile_n)
            first = jnp.dot(own_ref[...], acts[:half, cols], preferred_element_type=F32)
            second = jnp.dot(sib_ref[...], acts[half:, cols], preferred_element_type=F32)
            out_ref[:, cols] = ((first * first + second * second) * (1.0 / SEQS)).astype(BF16)

    return pl.pallas_call(
        kernel,
        grid_spec=pltpu.PrefetchScalarGridSpec(
            num_scalar_prefetch=1,
            grid=(out_rows // tile_o,),
            in_specs=[pl.BlockSpec((tile_o, seq_tokens), lambda o, place: (o, 0))] * 2
            + [IN_VMEM] * count,
            out_specs=pl.BlockSpec((tile_o, width), lambda o, place: (o, 0)),
            scratch_shapes=[pltpu.VMEM((SEQS * seq_tokens, width), BF16)],
        ),
        out_shape=jax.ShapeDtypeStruct((out_rows, width), BF16),
        compiler_params=vmem(20),
        cost_estimate=pl.CostEstimate(
            flops=2 * out_rows * width * SEQS * seq_tokens,
            bytes_accessed=2 * out_rows * width,
            transcendentals=0,
        ),
        name="lambda_product",
    )(place, own, sib, *arrays)


def chip_ring(chips):
    order = list(range(1, chips, 2))
    order = [0] + order + [c for c in range(chips - 1, 0, -1) if c % 2 == 0]
    return {order[i]: order[(i + 1) % chips] for i in range(chips)}


def on_both_cores(pairs):
    return [(CORES * a + k, CORES * b + k) for a, b in pairs for k in range(CORES)]


def powers(n):
    return [1 << b for b in range(n.bit_length() - 1)]


def halves(x, upper):
    half = x.shape[0] // 2
    low, high = x[:half], x[half:]
    return jnp.where(upper, high, low), jnp.where(upper, low, high)


def joined(mine, theirs, upper):
    return jnp.where(
        upper,
        jnp.concatenate([theirs, mine], axis=0),
        jnp.concatenate([mine, theirs], axis=0),
    )


def token_chunks(chips):
    half = max(chips // 2, 1)
    return [c for c in (list(range(half)), list(range(half, chips))) if c]


def local(rows_n, cols_n, activations, act_basis, out_grads, grad_basis):
    chips = cols_n // CORES
    col = lax.axis_index("col")
    row = lax.axis_index("row")
    core = col & 1
    swap = lambda x: lax.ppermute(x, "col", [(c, c ^ 1) for c in range(cols_n)])
    trade = lambda x, bit: lax.ppermute(x, "row", [(r, r ^ bit) for r in range(rows_n)])
    bits = powers(rows_n)
    rank_bit = [jnp.reshape((row & b).astype(jnp.int32), (1,)) for b in bits]

    succ = chip_ring(chips)
    pred = {b: a for a, b in succ.items()}
    ring = on_both_cores(sorted(succ.items()))
    blocks = [activations]
    pairs = [(activations, swap(activations))]
    grads = copy_gate(out_grads, pairs[0][1])
    for bit in bits[:-1]:
        grads = joined(grads, trade(grads, bit), (row & bit) != 0)
    for s in range(1, chips):
        block = lax.ppermute(blocks[-1], "col", ring)
        if s == 1:
            block = gate(block, grads)
        blocks.append(block)
        pairs.append((block, swap(block)))

    chip_bits = powers(chips)
    chip_trade = lambda x, bit: lax.ppermute(
        x, "col", on_both_cores([(c, c ^ bit) for c in range(chips)])
    )
    upper_chip = (col & CORES) != 0

    width = act_basis.shape[1]
    chunks = token_chunks(chips)
    tasks = []
    for n in range(len(chunks)):
        for i, columns in enumerate(column_parts(width, 2)):
            tasks.append((n, columns, bits if i % 2 == 0 else bits[::-1]))
    second = [t[0] for t in tasks].index(len(chunks) - 1)
    results, halved, summed, before, given = [], [], [], [], []
    plus = lambda a, b: (a.astype(F32) + b.astype(F32)).astype(BF16)
    for at, (n, (start, wide), order) in enumerate(tasks):
        tokens = [b for s in chunks[n] for b in pairs[s]]
        if at == second - 1 and at > 0:
            before.append(blocks[chips // 2])
        if at == second:
            mine, away = halves(mine, upper_chip)
            away = gate(away.astype(BF16), blocks[-1])
            before.append(away)
            mine = mine + chip_trade(away, 1).astype(F32)
        keep, send = chunk_dot(
            rank_bit[bits.index(order[0])], tokens, act_basis, start, wide, before
        )
        before = [send]
        if at == 0:
            got = gate(trade(grads, bits[-1]), send)
            part = lax.dot_general(
                grad_basis,
                joined(grads, got, (row & bits[-1]) != 0),
                (((0,), (1,)), ((), ())),
                preferred_element_type=F32,
            )
            seq_tokens = part.shape[1] // SEQS
            seqs = [part[:, :seq_tokens], part[:, seq_tokens:]]
            mine = jnp.where(core == 0, seqs[0], seqs[1])
            theirs = jnp.where(core == 0, seqs[1], seqs[0]).astype(BF16)
            mine = mine + swap(theirs).astype(F32)
            before.append(theirs)
        if at == second:
            for bit in chip_bits[1:]:
                away = mine.astype(BF16)
                if bit == chip_bits[1]:
                    away = gate(away, send)
                    before.append(away)
                mine = mine + chip_trade(away, bit).astype(F32)
        for where, got, order_s in summed:
            done = gate(got, send)
            before.append(done)
            given.append(trade(done, order_s[0]))
            results.append((where, done, order_s, given[-1]))
        summed = []
        for where, got, order_h in halved:
            for bit in order_h[1:]:
                if bit == order_h[1]:
                    got = gate(got, send)
                    before.append(got)
                got = plus(got, trade(got, bit))
            summed.append((where, got, order_h))
        halved = [((n, start), plus(keep, trade(send, order[0])), order)]
    for where, got, order_h in halved:
        for bit in order_h[1:]:
            got = plus(got, trade(got, bit))
        summed.append((where, got, order_h))
    for where, done, order_s in summed:
        results.append((where, done, order_s, trade(done, order_s[0])))
    own = gate(mine.astype(BF16), summed[0][1])
    own = joined(own, gate(chip_trade(own, 1), done), upper_chip)
    sib = swap(own)

    table = []
    for r in range(rows_n):
        for c in range(cols_n):
            here, k = c // CORES, c % CORES
            place = []
            for s in range(chips):
                block = (here + k * (chips // SEQS)) % chips
                place.append([CORES * block + k, CORES * block + 1 - k])
                here = pred[here]
            flat = []
            for (n, _), _, order, _ in results:
                units = [u for s in chunks[n] for u in place[s]]
                half = len(units) // 2
                low, high = units[:half], units[half:]
                flat += high + low if r & order[0] else low + high
            table.append(flat)
    place = jnp.asarray(np.array(table, np.int32))
    place = lax.dynamic_index_in_dim(place, row * cols_n + col, 0, keepdims=False)
    parts = [(w[1], array) for w, done, _, got in results for array in (done, got)]
    return lambda_product(place, own, sib, parts, activations.shape[0], width)


def solution(mesh):
    rows_n, cols_n = mesh.shape["row"], mesh.shape["col"]

    def body(activations, act_basis, out_grads, grad_basis):
        return local(rows_n, cols_n, activations, act_basis, out_grads, grad_basis)

    return jax.shard_map(
        body,
        mesh=mesh,
        in_specs=(P("col", "row"), P("row", "col"), P("row", "col"), P("col", "row")),
        out_specs=P("row", "col"),
        check_vma=False,
    )
```

```python
import functools

import jax
import jax.numpy as jnp
import numpy as np
from jax import lax
from jax.experimental import pallas as pl
from jax.experimental.pallas import tpu as pltpu
from jax.sharding import PartitionSpec as P

SEQS = 2
CORES = 2
F32 = jnp.float32
BF16 = jnp.bfloat16
ANYWHERE = pl.BlockSpec(memory_space=pl.ANY)
IN_VMEM = pl.BlockSpec(memory_space=pltpu.VMEM)


def vmem(mib):
    return pltpu.CompilerParams(vmem_limit_bytes=mib * 2**20)


def largest_tile(size, unit, most):
    tile = unit
    for candidate in range(unit, most + 1, unit):
        if size % candidate == 0:
            tile = candidate
    return tile if size % tile == 0 else size


def column_parts(width):
    unit = width // 7 if width % (7 * 128) == 0 else width // 8
    return [(0, 4 * unit), (4 * unit, width - 4 * unit)]


def column_tile(start, width):
    for tile in (256, 128):
        if start % tile == 0 and width % tile == 0:
            return tile
    raise ValueError("columns")


NO_COST = pl.CostEstimate(flops=0, bytes_accessed=0, transcendentals=0)


def gates(arrays, *after):
    count = len(arrays)
    return pl.pallas_call(
        lambda *refs: None,
        in_specs=[ANYWHERE] * (count + len(after)),
        out_specs=[ANYWHERE] * count,
        out_shape=[jax.ShapeDtypeStruct(x.shape, x.dtype) for x in arrays],
        input_output_aliases={i: i for i in range(count)},
        compiler_params=vmem(1),
        cost_estimate=NO_COST,
        name="gates",
    )(*arrays, *after)


def gate(x, *after):
    return gates([x], *after)[0]


def copy_gate(x, after):
    def kernel(x_ref, after_ref, out_ref):
        out_ref[...] = x_ref[...]

    return pl.pallas_call(
        kernel,
        in_specs=[pl.BlockSpec(memory_space=pltpu.VMEM), ANYWHERE],
        out_specs=pl.BlockSpec(memory_space=pltpu.VMEM),
        out_shape=jax.ShapeDtypeStruct(x.shape, x.dtype),
        compiler_params=vmem(2),
        cost_estimate=NO_COST,
        name="copy_gate",
    )(x, after)


def chunk_dot(blocks, basis, start, width, after=(), upper=None):
    rows, depth = blocks[0].shape
    tokens = rows * len(blocks)
    tile = column_tile(start, width)
    first = start // tile
    count = len(blocks)
    outs = 1 if upper is None else 2
    if upper is None:
        upper = jnp.zeros((1,), jnp.int32)

    def kernel(upper_ref, *rest):
        block_refs, basis_ref = rest[:count], rest[count]
        out_refs, joint = rest[-1 - outs : -1], rest[-1]

        @pl.when(pl.program_id(0) == 0)
        def _():
            for i, block_ref in enumerate(block_refs):
                joint[i * rows : (i + 1) * rows, :] = block_ref[...]

        total = jnp.dot(joint[...], basis_ref[...], preferred_element_type=F32)
        total = total.astype(BF16)
        if outs == 1:
            out_refs[0][...] = total
        else:
            half = tokens // 2
            is_upper = upper_ref[0] != 0
            out_refs[0][...] = jnp.where(is_upper, total[half:], total[:half])
            out_refs[1][...] = jnp.where(is_upper, total[:half], total[half:])

    out_rows = tokens // outs
    return pl.pallas_call(
        kernel,
        grid_spec=pltpu.PrefetchScalarGridSpec(
            num_scalar_prefetch=1,
            grid=(width // tile,),
            in_specs=[IN_VMEM] * count
            + [pl.BlockSpec((depth, tile), lambda n, s: (0, first + n))]
            + [ANYWHERE] * len(after),
            out_specs=[pl.BlockSpec((out_rows, tile), lambda n, s: (0, n))] * outs,
            scratch_shapes=[pltpu.VMEM((tokens, depth), BF16)],
        ),
        out_shape=[jax.ShapeDtypeStruct((out_rows, width), BF16)] * outs,
        compiler_params=vmem(24),
        cost_estimate=pl.CostEstimate(
            flops=2 * tokens * depth * width,
            bytes_accessed=2 * depth * width,
            transcendentals=0,
        ),
        name="chunk_dot",
    )(upper, *blocks, basis, *after)


def lambda_product(place, own, sib, parts, unit, width):
    out_rows, seq_tokens = own.shape
    tile_o = largest_tile(out_rows, 128, 256)
    tile_n = largest_tile(width, 128, 512)
    starts = [start for start, _ in parts]
    arrays = [array for _, array in parts]
    count = len(arrays)

    def kernel(place_ref, own_ref, sib_ref, *rest):
        part_refs, out_ref, acts = rest[:count], rest[-2], rest[-1]

        @pl.when(pl.program_id(0) == 0)
        def _():
            at = 0
            for start, part in zip(starts, part_refs):
                cols = slice(start, start + part.shape[1])
                for h in range(part.shape[0] // unit):
                    rows = pl.ds(pl.multiple_of(place_ref[at] * unit, unit), unit)
                    acts[rows, cols] = part[h * unit : (h + 1) * unit, :]
                    at += 1

        half = acts.shape[0] // 2
        for start in range(0, width, tile_n):
            cols = pl.ds(start, tile_n)
            first = jnp.dot(own_ref[...], acts[:half, cols], preferred_element_type=F32)
            second = jnp.dot(sib_ref[...], acts[half:, cols], preferred_element_type=F32)
            out_ref[:, cols] = ((first * first + second * second) * (1.0 / SEQS)).astype(BF16)

    return pl.pallas_call(
        kernel,
        grid_spec=pltpu.PrefetchScalarGridSpec(
            num_scalar_prefetch=1,
            grid=(out_rows // tile_o,),
            in_specs=[pl.BlockSpec((tile_o, seq_tokens), lambda o, place: (o, 0))] * 2
            + [IN_VMEM] * count,
            out_specs=pl.BlockSpec((tile_o, width), lambda o, place: (o, 0)),
            scratch_shapes=[pltpu.VMEM((SEQS * seq_tokens, width), BF16)],
        ),
        out_shape=jax.ShapeDtypeStruct((out_rows, width), BF16),
        compiler_params=vmem(20),
        cost_estimate=pl.CostEstimate(
            flops=2 * out_rows * width * SEQS * seq_tokens,
            bytes_accessed=2 * out_rows * width,
            transcendentals=0,
        ),
        name="lambda_product",
    )(place, own, sib, *arrays)


def chip_ring(chips):
    order = list(range(1, chips, 2))
    order = [0] + order + [c for c in range(chips - 1, 0, -1) if c % 2 == 0]
    return {order[i]: order[(i + 1) % chips] for i in range(chips)}


def on_both_cores(pairs):
    return [(CORES * a + k, CORES * b + k) for a, b in pairs for k in range(CORES)]


def powers(n):
    return [1 << b for b in range(n.bit_length() - 1)]


def halves(x, upper):
    half = x.shape[0] // 2
    low, high = x[:half], x[half:]
    return jnp.where(upper, high, low), jnp.where(upper, low, high)


def joined(mine, theirs, upper):
    return jnp.where(
        upper,
        jnp.concatenate([theirs, mine], axis=0),
        jnp.concatenate([mine, theirs], axis=0),
    )


def local(rows_n, cols_n, activations, act_basis, out_grads, grad_basis):
    chips = cols_n // CORES
    col = lax.axis_index("col")
    row = lax.axis_index("row")
    core = col & 1
    swap = lambda x: lax.ppermute(x, "col", [(c, c ^ 1) for c in range(cols_n)])
    trade = lambda x, bit: lax.ppermute(x, "row", [(r, r ^ bit) for r in range(rows_n)])
    bits = powers(rows_n)
    rank_bit = [jnp.reshape((row & b).astype(jnp.int32), (1,)) for b in bits]

    succ = chip_ring(chips)
    pred = {b: a for a, b in succ.items()}
    ring = on_both_cores(sorted(succ.items()))
    blocks = [activations]
    pairs = [(activations, swap(activations))]
    grads = copy_gate(out_grads, pairs[0][1])
    for bit in bits[:-1]:
        grads = joined(grads, trade(grads, bit), (row & bit) != 0)
    for s in range(1, chips):
        block = lax.ppermute(blocks[-1], "col", ring)
        if s == 1:
            block = gate(block, grads)
        blocks.append(block)
        pairs.append((block, swap(block)))

    chip_bits = powers(chips)
    chip_trade = lambda x, bit: lax.ppermute(
        x, "col", on_both_cores([(c, c ^ bit) for c in range(chips)])
    )
    upper_chip = (col & CORES) != 0
    plus = lambda a, b: (a.astype(F32) + b.astype(F32)).astype(BF16)
    bit0 = bits[0]

    def plus_others(x, got):
        x = plus(x, got)
        for bit in bits[2:]:
            x = plus(x, trade(x, bit))
        return x

    half = chips // 2
    width = act_basis.shape[1]
    (start_l, wide_l), (start_r, wide_r) = column_parts(width)
    early = [b for p in pairs[:half] for b in p]
    late = [b for p in pairs[half:] for b in p]

    (part_l,) = chunk_dot(early, act_basis, start_l, wide_l)
    first_l = trade(part_l, bit0)
    got = gate(trade(grads, bits[-1]), part_l)
    part = lax.dot_general(
        grad_basis,
        joined(grads, got, (row & bits[-1]) != 0),
        (((0,), (1,)), ((), ())),
        preferred_element_type=F32,
    )
    seq_tokens = part.shape[1] // SEQS
    seqs = [part[:, :seq_tokens], part[:, seq_tokens:]]
    mine = jnp.where(core == 0, seqs[0], seqs[1])
    theirs = jnp.where(core == 0, seqs[1], seqs[0]).astype(BF16)
    mine = mine + swap(theirs).astype(F32)
    mine, away = halves(mine, upper_chip)
    (part_r,) = chunk_dot(early, act_basis, start_r, wide_r, (blocks[half], theirs))

    sum_l = plus(part_l, first_l)
    part_r, sum_l, away = gates([part_r, sum_l, away.astype(BF16)])
    first_r = trade(part_r, bit0)
    second_l = trade(sum_l, bits[1])
    mine = mine + chip_trade(away, 1).astype(F32)
    upper = rank_bit[0]
    keep_l, send_l = chunk_dot(late, act_basis, start_l, wide_l, (part_r,), upper)

    sum_r = plus(part_r, first_r)
    early_l = plus_others(sum_l, second_l)
    send_l, sum_r, away = gates([send_l, sum_r, mine.astype(BF16)], early_l)
    second_r = trade(sum_r, bits[1])
    got_l = trade(send_l, bit0)
    for bit in chip_bits[1:]:
        mine = mine + chip_trade(away, bit).astype(F32)
        away = mine.astype(BF16)
    keep_r, send_r = chunk_dot(late, act_basis, start_r, wide_r, (send_l,), upper)

    early_r = plus_others(sum_r, second_r)
    send_r, keep_l = gates([send_r, plus(keep_l, got_l)], early_r)
    got_r = trade(send_r, bit0)
    got_l = trade(keep_l, bits[1])

    late_l = plus_others(keep_l, got_l)
    late_l, keep_r, own = gates([late_l, plus(keep_r, got_r), away])
    other_l = trade(late_l, bit0)
    got_r = trade(keep_r, bits[1])
    other_own = chip_trade(own, 1)

    late_r = plus_others(keep_r, got_r)
    late_r, own = gates([late_r, joined(own, other_own, upper_chip)], other_l)
    other_r = trade(late_r, bit0)
    sib = swap(own)

    table = []
    for r in range(rows_n):
        for c in range(cols_n):
            here, k = c // CORES, c % CORES
            place = []
            for _ in range(chips):
                block = (here + k * (chips // SEQS)) % chips
                place += [CORES * block + k, CORES * block + 1 - k]
                here = pred[here]
            first, low, high = place[:chips], place[chips:][:half], place[chips:][half:]
            last = high + low if r & bit0 else low + high
            table.append(first + first + last + last)
    place = jnp.asarray(np.array(table, np.int32))
    place = lax.dynamic_index_in_dim(place, row * cols_n + col, 0, keepdims=False)
    parts = [(start_l, early_l), (start_r, early_r)]
    parts += [(start_l, late_l), (start_l, other_l), (start_r, late_r), (start_r, other_r)]
    return lambda_product(place, own, sib, parts, activations.shape[0], width)


def solution(mesh):
    rows_n, cols_n = mesh.shape["row"], mesh.shape["col"]

    def body(activations, act_basis, out_grads, grad_basis):
        return local(rows_n, cols_n, activations, act_basis, out_grads, grad_basis)

    return jax.shard_map(
        body,
        mesh=mesh,
        in_specs=(P("col", "row"), P("row", "col"), P("row", "col"), P("col", "row")),
        out_specs=P("row", "col"),
        check_vma=False,
    )
```

```python
import functools

import jax
import jax.numpy as jnp
import numpy as np
from jax import lax
from jax.experimental import pallas as pl
from jax.experimental.pallas import tpu as pltpu
from jax.sharding import PartitionSpec as P

SEQS = 2
CORES = 2
F32 = jnp.float32
BF16 = jnp.bfloat16
ANYWHERE = pl.BlockSpec(memory_space=pl.ANY)
IN_VMEM = pl.BlockSpec(memory_space=pltpu.VMEM)


def vmem(mib):
    return pltpu.CompilerParams(vmem_limit_bytes=mib * 2**20)


def largest_tile(size, unit, most):
    tile = unit
    for candidate in range(unit, most + 1, unit):
        if size % candidate == 0:
            tile = candidate
    return tile if size % tile == 0 else size


def column_parts(width):
    unit = width // 7 if width % (7 * 128) == 0 else width // 8
    return [(0, 4 * unit), (4 * unit, width - 4 * unit)]


def column_tile(start, width, most=256):
    for tile in (512, 256, 128):
        if tile <= most and start % tile == 0 and width % tile == 0:
            return tile
    raise ValueError("columns")


NO_COST = pl.CostEstimate(flops=0, bytes_accessed=0, transcendentals=0)


def gates(arrays, *after):
    count = len(arrays)
    return pl.pallas_call(
        lambda *refs: None,
        in_specs=[ANYWHERE] * (count + len(after)),
        out_specs=[ANYWHERE] * count,
        out_shape=[jax.ShapeDtypeStruct(x.shape, x.dtype) for x in arrays],
        input_output_aliases={i: i for i in range(count)},
        compiler_params=vmem(1),
        cost_estimate=NO_COST,
        name="gates",
    )(*arrays, *after)


def gate(x, *after):
    return gates([x], *after)[0]


def copy_gate(x, after):
    def kernel(x_ref, after_ref, out_ref):
        out_ref[...] = x_ref[...]

    return pl.pallas_call(
        kernel,
        in_specs=[pl.BlockSpec(memory_space=pltpu.VMEM), ANYWHERE],
        out_specs=pl.BlockSpec(memory_space=pltpu.VMEM),
        out_shape=jax.ShapeDtypeStruct(x.shape, x.dtype),
        compiler_params=vmem(2),
        cost_estimate=NO_COST,
        name="copy_gate",
    )(x, after)


def chunk_dot(blocks, basis, start, width, after=(), upper=None):
    rows, depth = blocks[0].shape
    tokens = rows * len(blocks)
    tile = column_tile(start, width)
    first = start // tile
    count = len(blocks)
    outs = 1 if upper is None else 2
    if upper is None:
        upper = jnp.zeros((1,), jnp.int32)

    def kernel(upper_ref, *rest):
        block_refs, basis_ref = rest[:count], rest[count]
        out_refs, joint = rest[-1 - outs : -1], rest[-1]

        @pl.when(pl.program_id(0) == 0)
        def _():
            for i, block_ref in enumerate(block_refs):
                joint[i * rows : (i + 1) * rows, :] = block_ref[...]

        total = jnp.dot(joint[...], basis_ref[...], preferred_element_type=F32)
        total = total.astype(BF16)
        if outs == 1:
            out_refs[0][...] = total
        else:
            half = tokens // 2
            is_upper = upper_ref[0] != 0
            out_refs[0][...] = jnp.where(is_upper, total[half:], total[:half])
            out_refs[1][...] = jnp.where(is_upper, total[:half], total[half:])

    out_rows = tokens // outs
    return pl.pallas_call(
        kernel,
        grid_spec=pltpu.PrefetchScalarGridSpec(
            num_scalar_prefetch=1,
            grid=(width // tile,),
            in_specs=[IN_VMEM] * count
            + [pl.BlockSpec((depth, tile), lambda n, s: (0, first + n))]
            + [ANYWHERE] * len(after),
            out_specs=[pl.BlockSpec((out_rows, tile), lambda n, s: (0, n))] * outs,
            scratch_shapes=[pltpu.VMEM((tokens, depth), BF16)],
        ),
        out_shape=[jax.ShapeDtypeStruct((out_rows, width), BF16)] * outs,
        compiler_params=vmem(16),
        cost_estimate=pl.CostEstimate(
            flops=2 * tokens * depth * width,
            bytes_accessed=2 * depth * width,
            transcendentals=0,
        ),
        name="chunk_dot",
    )(upper, *blocks, basis, *after)


def lambda_product(place, own, sib, parts, unit, start, width, whole, so_far=None):
    out_rows, seq_tokens = own.shape
    tile_o = largest_tile(out_rows, 128, 512)
    tile_n = column_tile(start, width, 512)
    inner = min(tile_n, 256)
    first_tile = start // tile_n
    count = len(parts)
    given = [] if so_far is None else [so_far]

    def kernel(place_ref, own_ref, sib_ref, *rest):
        part_refs, out_ref, acts = rest[:count], rest[-2], rest[-1]
        n, o = pl.program_id(0), pl.program_id(1)

        @pl.when(jnp.logical_and(n == 0, o == 0))
        def _():
            at = 0
            for part in part_refs:
                for h in range(part.shape[0] // unit):
                    rows = pl.ds(pl.multiple_of(place_ref[at] * unit, unit), unit)
                    acts[rows, :] = part[h * unit : (h + 1) * unit, :]
                    at += 1

        rows = pl.ds(pl.multiple_of(o * tile_o, tile_o), tile_o)
        for i in range(tile_n // inner):
            cols = pl.ds(pl.multiple_of(n * tile_n + i * inner, inner), inner)
            first = jnp.dot(
                own_ref[rows, :], acts[:seq_tokens, cols], preferred_element_type=F32
            )
            second = jnp.dot(
                sib_ref[rows, :], acts[seq_tokens:, cols], preferred_element_type=F32
            )
            mean = (first * first + second * second) * (1.0 / SEQS)
            out_ref[:, i * inner : (i + 1) * inner] = mean.astype(BF16)

    return pl.pallas_call(
        kernel,
        grid_spec=pltpu.PrefetchScalarGridSpec(
            num_scalar_prefetch=1,
            grid=(width // tile_n, out_rows // tile_o),
            in_specs=[IN_VMEM] * (2 + count) + [ANYWHERE] * len(given),
            out_specs=pl.BlockSpec((tile_o, tile_n), lambda n, o, s: (o, first_tile + n)),
            scratch_shapes=[pltpu.VMEM((SEQS * seq_tokens, width), BF16)],
        ),
        out_shape=jax.ShapeDtypeStruct((out_rows, whole), BF16),
        input_output_aliases={3 + count: 0} if given else {},
        compiler_params=vmem(12),
        cost_estimate=pl.CostEstimate(
            flops=2 * out_rows * width * SEQS * seq_tokens,
            bytes_accessed=2 * out_rows * width,
            transcendentals=0,
        ),
        name="lambda_product",
    )(place, own, sib, *parts, *given)


def chip_ring(chips):
    order = list(range(1, chips, 2))
    order = [0] + order + [c for c in range(chips - 1, 0, -1) if c % 2 == 0]
    return {order[i]: order[(i + 1) % chips] for i in range(chips)}


def on_both_cores(pairs):
    return [(CORES * a + k, CORES * b + k) for a, b in pairs for k in range(CORES)]


def powers(n):
    return [1 << b for b in range(n.bit_length() - 1)]


def halves(x, upper):
    half = x.shape[0] // 2
    low, high = x[:half], x[half:]
    return jnp.where(upper, high, low), jnp.where(upper, low, high)


def joined(mine, theirs, upper):
    return jnp.where(
        upper,
        jnp.concatenate([theirs, mine], axis=0),
        jnp.concatenate([mine, theirs], axis=0),
    )


def local(rows_n, cols_n, activations, act_basis, out_grads, grad_basis):
    chips = cols_n // CORES
    col = lax.axis_index("col")
    row = lax.axis_index("row")
    core = col & 1
    swap = lambda x: lax.ppermute(x, "col", [(c, c ^ 1) for c in range(cols_n)])
    trade = lambda x, bit: lax.ppermute(x, "row", [(r, r ^ bit) for r in range(rows_n)])
    bits = powers(rows_n)
    rank_bit = [jnp.reshape((row & b).astype(jnp.int32), (1,)) for b in bits]

    succ = chip_ring(chips)
    pred = {b: a for a, b in succ.items()}
    ring = on_both_cores(sorted(succ.items()))
    blocks = [activations]
    pairs = [(activations, swap(activations))]
    grads = copy_gate(out_grads, pairs[0][1])
    pieces = [grads] + [trade(grads, mask) for mask in range(1, rows_n)]
    for bit in bits:
        pieces = [
            joined(low, high, (row & bit) != 0)
            for low, high in zip(pieces[::2], pieces[1::2])
        ]
    grads = pieces[0]
    for s in range(1, chips):
        block = lax.ppermute(blocks[-1], "col", ring)
        if s == 1:
            block = gate(block, grads)
        blocks.append(block)
        pairs.append((block, swap(block)))

    chip_bits = powers(chips)
    chip_trade = lambda x, bit: lax.ppermute(
        x, "col", on_both_cores([(c, c ^ bit) for c in range(chips)])
    )
    upper_chip = (col & CORES) != 0
    plus = lambda a, b: (a.astype(F32) + b.astype(F32)).astype(BF16)
    bit0 = bits[0]

    def plus_others(x, got):
        x = plus(x, got)
        for bit in bits[2:]:
            x = plus(x, trade(x, bit))
        return x

    half = chips // 2
    width = act_basis.shape[1]
    (start_l, wide_l), (start_r, wide_r) = column_parts(width)
    early = [b for p in pairs[:half] for b in p]
    late = [b for p in pairs[half:] for b in p]

    part = lax.dot_general(
        grad_basis,
        grads,
        (((0,), (1,)), ((), ())),
        preferred_element_type=F32,
    )
    seq_tokens = part.shape[1] // SEQS
    seqs = [part[:, :seq_tokens], part[:, seq_tokens:]]
    mine = jnp.where(core == 0, seqs[0], seqs[1])
    theirs = jnp.where(core == 0, seqs[1], seqs[0]).astype(BF16)
    mine = mine + swap(theirs).astype(F32)
    mine, away = halves(mine, upper_chip)

    (part_l,) = chunk_dot(early, act_basis, start_l, wide_l, (theirs,))
    first_l = trade(part_l, bit0)
    (part_r,) = chunk_dot(early, act_basis, start_r, wide_r, (blocks[half], part_l))
    sum_l = plus(part_l, first_l)
    part_r, sum_l, away = gates([part_r, sum_l, away.astype(BF16)])
    first_r = trade(part_r, bit0)
    second_l = trade(sum_l, bits[1])
    first_away = chip_trade(away, 1)
    upper = rank_bit[0]
    keep_l, send_l = chunk_dot(late, act_basis, start_l, wide_l, (part_r,), upper)

    first_r, second_l, first_away = gates([first_r, second_l, first_away], send_l)
    mine = mine + first_away.astype(F32)
    sum_r = plus(part_r, first_r)
    early_l = plus_others(sum_l, second_l)
    send_l, sum_r, away = gates([send_l, sum_r, mine.astype(BF16)], early_l)
    second_r = trade(sum_r, bits[1])
    got_l = trade(send_l, bit0)
    for bit in chip_bits[1:]:
        mine = mine + chip_trade(away, bit).astype(F32)
        away = mine.astype(BF16)
    keep_r, send_r = chunk_dot(late, act_basis, start_r, wide_r, (send_l,), upper)

    early_r = plus_others(sum_r, second_r)
    send_r, keep_l = gates([send_r, plus(keep_l, got_l)], early_r)
    got_r = trade(send_r, bit0)
    got_l = trade(keep_l, bits[1])

    late_l = plus_others(keep_l, got_l)
    late_l, keep_r, own = gates([late_l, plus(keep_r, got_r), away])
    other_l = trade(late_l, bit0)
    got_r = trade(keep_r, bits[1])
    other_own = chip_trade(own, 1)

    late_r = plus_others(keep_r, got_r)
    late_r, own = gates([late_r, joined(own, other_own, upper_chip)], other_l)
    other_r = trade(late_r, bit0)
    sib = swap(own)

    table = []
    for r in range(rows_n):
        for c in range(cols_n):
            here, k = c // CORES, c % CORES
            place = []
            for _ in range(chips):
                block = (here + k * (chips // SEQS)) % chips
                place += [CORES * block + k, CORES * block + 1 - k]
                here = pred[here]
            first, low, high = place[:chips], place[chips:][:half], place[chips:][half:]
            last = high + low if r & bit0 else low + high
            table.append(first + last)
    place = jnp.asarray(np.array(table, np.int32))
    place = lax.dynamic_index_in_dim(place, row * cols_n + col, 0, keepdims=False)
    unit = activations.shape[0]
    parts_l = [early_l, late_l, other_l]
    out = lambda_product(place, own, sib, parts_l, unit, start_l, wide_l, width)
    parts_r = [early_r, late_r, other_r]
    return lambda_product(place, own, sib, parts_r, unit, start_r, wide_r, width, out)


def solution(mesh):
    rows_n, cols_n = mesh.shape["row"], mesh.shape["col"]

    def body(activations, act_basis, out_grads, grad_basis):
        return local(rows_n, cols_n, activations, act_basis, out_grads, grad_basis)

    return jax.shard_map(
        body,
        mesh=mesh,
        in_specs=(P("col", "row"), P("row", "col"), P("row", "col"), P("col", "row")),
        out_specs=P("row", "col"),
        check_vma=False,
    )
```

```python
import functools

import jax
import jax.numpy as jnp
import numpy as np
from jax import lax
from jax.experimental import pallas as pl
from jax.experimental.pallas import tpu as pltpu
from jax.sharding import PartitionSpec as P

SEQS = 2
CORES = 2
F32 = jnp.float32
BF16 = jnp.bfloat16
ANYWHERE = pl.BlockSpec(memory_space=pl.ANY)
IN_VMEM = pl.BlockSpec(memory_space=pltpu.VMEM)


def vmem(mib):
    return pltpu.CompilerParams(vmem_limit_bytes=mib * 2**20)


def largest_tile(size, unit, most):
    tile = unit
    for candidate in range(unit, most + 1, unit):
        if size % candidate == 0:
            tile = candidate
    return tile if size % tile == 0 else size


def column_parts(width):
    right = width // 2 if width % 512 == 0 else 128
    return [(0, width - right), (width - right, right)]


def column_tile(start, width, most=256):
    for tile in (512, 256, 128):
        if tile <= most and start % tile == 0 and width % tile == 0:
            return tile
    raise ValueError("columns")


NO_COST = pl.CostEstimate(flops=0, bytes_accessed=0, transcendentals=0)


def gates(arrays, *after):
    count = len(arrays)
    return pl.pallas_call(
        lambda *refs: None,
        in_specs=[ANYWHERE] * (count + len(after)),
        out_specs=[ANYWHERE] * count,
        out_shape=[jax.ShapeDtypeStruct(x.shape, x.dtype) for x in arrays],
        input_output_aliases={i: i for i in range(count)},
        compiler_params=vmem(1),
        cost_estimate=NO_COST,
        name="gates",
    )(*arrays, *after)


def gate(x, *after):
    return gates([x], *after)[0]


def copy_gate(x, after):
    def kernel(x_ref, after_ref, out_ref):
        out_ref[...] = x_ref[...]

    return pl.pallas_call(
        kernel,
        in_specs=[pl.BlockSpec(memory_space=pltpu.VMEM), ANYWHERE],
        out_specs=pl.BlockSpec(memory_space=pltpu.VMEM),
        out_shape=jax.ShapeDtypeStruct(x.shape, x.dtype),
        compiler_params=vmem(2),
        cost_estimate=NO_COST,
        name="copy_gate",
    )(x, after)


def chunk_dot(blocks, basis, start, width, after=(), upper=None):
    rows, depth = blocks[0].shape
    tokens = rows * len(blocks)
    tile = column_tile(start, width)
    first = start // tile
    count = len(blocks)
    outs = 1 if upper is None else 2
    if upper is None:
        upper = jnp.zeros((1,), jnp.int32)

    def kernel(upper_ref, *rest):
        block_refs, basis_ref = rest[:count], rest[count]
        out_refs, joint = rest[-1 - outs : -1], rest[-1]

        @pl.when(pl.program_id(0) == 0)
        def _():
            for i, block_ref in enumerate(block_refs):
                joint[i * rows : (i + 1) * rows, :] = block_ref[...]

        total = jnp.dot(joint[...], basis_ref[...], preferred_element_type=F32)
        total = total.astype(BF16)
        if outs == 1:
            out_refs[0][...] = total
        else:
            half = tokens // 2
            is_upper = upper_ref[0] != 0
            out_refs[0][...] = jnp.where(is_upper, total[half:], total[:half])
            out_refs[1][...] = jnp.where(is_upper, total[:half], total[half:])

    out_rows = tokens // outs
    return pl.pallas_call(
        kernel,
        grid_spec=pltpu.PrefetchScalarGridSpec(
            num_scalar_prefetch=1,
            grid=(width // tile,),
            in_specs=[IN_VMEM] * count
            + [pl.BlockSpec((depth, tile), lambda n, s: (0, first + n))]
            + [ANYWHERE] * len(after),
            out_specs=[pl.BlockSpec((out_rows, tile), lambda n, s: (0, n))] * outs,
            scratch_shapes=[pltpu.VMEM((tokens, depth), BF16)],
        ),
        out_shape=[jax.ShapeDtypeStruct((out_rows, width), BF16)] * outs,
        compiler_params=vmem(16),
        cost_estimate=pl.CostEstimate(
            flops=2 * tokens * depth * width,
            bytes_accessed=2 * depth * width,
            transcendentals=0,
        ),
        name="chunk_dot",
    )(upper, *blocks, basis, *after)


def lambda_product(place, own, sib, parts, unit, start, width, whole, so_far=None):
    out_rows, seq_tokens = own.shape
    tile_o = largest_tile(out_rows, 128, 256)
    tile_n = 256 if width % 256 == 0 else 128
    at_block = start // width
    count = len(parts)
    given = [] if so_far is None else [so_far]

    def kernel(place_ref, own_ref, sib_ref, *rest):
        part_refs, out_ref, acts = rest[:count], rest[-2], rest[-1]

        @pl.when(pl.program_id(0) == 0)
        def _():
            at = 0
            for part in part_refs:
                for h in range(part.shape[0] // unit):
                    rows = pl.ds(pl.multiple_of(place_ref[at] * unit, unit), unit)
                    acts[rows, :] = part[h * unit : (h + 1) * unit, :]
                    at += 1

        for n in range(0, width, tile_n):
            cols = pl.ds(n, tile_n)
            first = jnp.dot(own_ref[...], acts[:seq_tokens, cols], preferred_element_type=F32)
            second = jnp.dot(sib_ref[...], acts[seq_tokens:, cols], preferred_element_type=F32)
            mean = (first * first + second * second) * (1.0 / SEQS)
            out_ref[:, cols] = mean.astype(BF16)

    return pl.pallas_call(
        kernel,
        grid_spec=pltpu.PrefetchScalarGridSpec(
            num_scalar_prefetch=1,
            grid=(out_rows // tile_o,),
            in_specs=[pl.BlockSpec((tile_o, seq_tokens), lambda o, s: (o, 0))] * 2
            + [IN_VMEM] * count
            + [ANYWHERE] * len(given),
            out_specs=pl.BlockSpec((tile_o, width), lambda o, s: (o, at_block)),
            scratch_shapes=[pltpu.VMEM((SEQS * seq_tokens, width), BF16)],
        ),
        out_shape=jax.ShapeDtypeStruct((out_rows, whole), BF16),
        input_output_aliases={3 + count: 0} if given else {},
        compiler_params=vmem(12),
        cost_estimate=pl.CostEstimate(
            flops=2 * out_rows * width * SEQS * seq_tokens,
            bytes_accessed=2 * out_rows * width,
            transcendentals=0,
        ),
        name="lambda_product",
    )(place, own, sib, *parts, *given)


def chip_ring(chips):
    order = list(range(1, chips, 2))
    order = [0] + order + [c for c in range(chips - 1, 0, -1) if c % 2 == 0]
    return {order[i]: order[(i + 1) % chips] for i in range(chips)}


def on_both_cores(pairs):
    return [(CORES * a + k, CORES * b + k) for a, b in pairs for k in range(CORES)]


def powers(n):
    return [1 << b for b in range(n.bit_length() - 1)]


def halves(x, upper):
    half = x.shape[0] // 2
    low, high = x[:half], x[half:]
    return jnp.where(upper, high, low), jnp.where(upper, low, high)


def joined(mine, theirs, upper):
    return jnp.where(
        upper,
        jnp.concatenate([theirs, mine], axis=0),
        jnp.concatenate([mine, theirs], axis=0),
    )


def local(rows_n, cols_n, activations, act_basis, out_grads, grad_basis):
    chips = cols_n // CORES
    col = lax.axis_index("col")
    row = lax.axis_index("row")
    core = col & 1
    swap = lambda x: lax.ppermute(x, "col", [(c, c ^ 1) for c in range(cols_n)])
    trade = lambda x, bit: lax.ppermute(x, "row", [(r, r ^ bit) for r in range(rows_n)])
    bits = powers(rows_n)
    rank_bit = [jnp.reshape((row & b).astype(jnp.int32), (1,)) for b in bits]

    succ = chip_ring(chips)
    pred = {b: a for a, b in succ.items()}
    ring = on_both_cores(sorted(succ.items()))
    blocks = [activations]
    pairs = [(activations, swap(activations))]
    grads = copy_gate(out_grads, pairs[0][1])
    pieces = [grads] + [trade(grads, mask) for mask in range(1, rows_n)]
    for bit in bits:
        pieces = [
            joined(low, high, (row & bit) != 0)
            for low, high in zip(pieces[::2], pieces[1::2])
        ]
    grads = pieces[0]
    for s in range(1, chips):
        block = lax.ppermute(blocks[-1], "col", ring)
        if s == 1:
            block = gate(block, grads)
        blocks.append(block)
        pairs.append((block, swap(block)))

    chip_bits = powers(chips)
    chip_trade = lambda x, bit: lax.ppermute(
        x, "col", on_both_cores([(c, c ^ bit) for c in range(chips)])
    )
    upper_chip = (col & CORES) != 0
    plus = lambda a, b: (a.astype(F32) + b.astype(F32)).astype(BF16)
    bit0 = bits[0]

    def plus_others(x, got):
        x = plus(x, got)
        for bit in bits[2:]:
            x = plus(x, trade(x, bit))
        return x

    half = chips // 2
    width = act_basis.shape[1]
    (start_l, wide_l), (start_r, wide_r) = column_parts(width)
    early = [b for p in pairs[:half] for b in p]
    late = [b for p in pairs[half:] for b in p]

    part = lax.dot_general(
        grad_basis,
        grads,
        (((0,), (1,)), ((), ())),
        preferred_element_type=F32,
    )
    seq_tokens = part.shape[1] // SEQS
    seqs = [part[:, :seq_tokens], part[:, seq_tokens:]]
    mine = jnp.where(core == 0, seqs[0], seqs[1])
    theirs = jnp.where(core == 0, seqs[1], seqs[0]).astype(BF16)
    mine = mine + swap(theirs).astype(F32)
    mine, away = halves(mine, upper_chip)

    part_l = jnp.dot(
        gate(jnp.concatenate(early, axis=0), theirs),
        act_basis[:, :wide_l],
        preferred_element_type=F32,
    ).astype(BF16)
    first_l = trade(part_l, bit0)
    (part_r,) = chunk_dot(early, act_basis, start_r, wide_r, (blocks[half], part_l))
    sum_l = plus(part_l, first_l)
    part_r, sum_l, away = gates([part_r, sum_l, away.astype(BF16)])
    first_r = trade(part_r, bit0)
    second_l = trade(sum_l, bits[1])
    first_away = chip_trade(away, 1)
    upper = rank_bit[0]
    keep_l, send_l = chunk_dot(late, act_basis, start_l, wide_l, (part_r,), upper)

    first_r, second_l, first_away = gates([first_r, second_l, first_away], send_l)
    mine = mine + first_away.astype(F32)
    sum_r = plus(part_r, first_r)
    early_l = plus_others(sum_l, second_l)
    send_l, sum_r, away = gates([send_l, sum_r, mine.astype(BF16)], early_l)
    second_r = trade(sum_r, bits[1])
    got_l = trade(send_l, bit0)
    for bit in chip_bits[1:]:
        mine = mine + chip_trade(away, bit).astype(F32)
        away = mine.astype(BF16)
    keep_r, send_r = chunk_dot(late, act_basis, start_r, wide_r, (send_l,), upper)

    early_r = plus_others(sum_r, second_r)
    send_r, keep_l = gates([send_r, plus(keep_l, got_l)], early_r)
    got_r = trade(send_r, bit0)
    got_l = trade(keep_l, bits[1])

    late_l = plus_others(keep_l, got_l)
    late_l, keep_r, own = gates([late_l, plus(keep_r, got_r), away])
    other_l = trade(late_l, bit0)
    got_r = trade(keep_r, bits[1])
    other_own = chip_trade(own, 1)

    late_r = plus_others(keep_r, got_r)
    late_r, own = gates([late_r, joined(own, other_own, upper_chip)], other_l)
    other_r = trade(late_r, bit0)
    sib = swap(own)

    table = []
    for r in range(rows_n):
        for c in range(cols_n):
            here, k = c // CORES, c % CORES
            place = []
            for _ in range(chips):
                block = (here + k * (chips // SEQS)) % chips
                place += [CORES * block + k, CORES * block + 1 - k]
                here = pred[here]
            first, low, high = place[:chips], place[chips:][:half], place[chips:][half:]
            last = high + low if r & bit0 else low + high
            table.append(first + last)
    place = jnp.asarray(np.array(table, np.int32))
    place = lax.dynamic_index_in_dim(place, row * cols_n + col, 0, keepdims=False)
    unit = activations.shape[0]
    parts_l = [early_l, late_l, other_l]
    out = lambda_product(place, own, sib, parts_l, unit, start_l, wide_l, width)
    parts_r = [early_r, late_r, other_r]
    return lambda_product(place, own, sib, parts_r, unit, start_r, wide_r, width, out)


def solution(mesh):
    rows_n, cols_n = mesh.shape["row"], mesh.shape["col"]

    def body(activations, act_basis, out_grads, grad_basis):
        return local(rows_n, cols_n, activations, act_basis, out_grads, grad_basis)

    return jax.shard_map(
        body,
        mesh=mesh,
        in_specs=(P("col", "row"), P("row", "col"), P("row", "col"), P("col", "row")),
        out_specs=P("row", "col"),
        check_vma=False,
    )
```

```python
import functools

import jax
import jax.numpy as jnp
import numpy as np
from jax import lax
from jax.experimental import pallas as pl
from jax.experimental.pallas import tpu as pltpu
from jax.sharding import PartitionSpec as P

SEQS = 2
CORES = 2
F32 = jnp.float32
BF16 = jnp.bfloat16
ANYWHERE = pl.BlockSpec(memory_space=pl.ANY)
IN_VMEM = pl.BlockSpec(memory_space=pltpu.VMEM)


def vmem(mib):
    return pltpu.CompilerParams(vmem_limit_bytes=mib * 2**20)


def largest_tile(size, unit, most):
    tile = unit
    for candidate in range(unit, most + 1, unit):
        if size % candidate == 0:
            tile = candidate
    return tile if size % tile == 0 else size


def column_parts(width):
    right = width // 2 if width % 512 == 0 else 128
    return [(0, width - right), (width - right, right)]


NO_COST = pl.CostEstimate(flops=0, bytes_accessed=0, transcendentals=0)


def gates(arrays, *after):
    count = len(arrays)
    return pl.pallas_call(
        lambda *refs: None,
        in_specs=[ANYWHERE] * (count + len(after)),
        out_specs=[ANYWHERE] * count,
        out_shape=[jax.ShapeDtypeStruct(x.shape, x.dtype) for x in arrays],
        input_output_aliases={i: i for i in range(count)},
        compiler_params=vmem(1),
        cost_estimate=NO_COST,
        name="gates",
    )(*arrays, *after)


def gate(x, *after):
    return gates([x], *after)[0]


def copy_gate(x, after):
    def kernel(x_ref, after_ref, out_ref):
        out_ref[...] = x_ref[...]

    return pl.pallas_call(
        kernel,
        in_specs=[pl.BlockSpec(memory_space=pltpu.VMEM), ANYWHERE],
        out_specs=pl.BlockSpec(memory_space=pltpu.VMEM),
        out_shape=jax.ShapeDtypeStruct(x.shape, x.dtype),
        compiler_params=vmem(2),
        cost_estimate=NO_COST,
        name="copy_gate",
    )(x, after)


def chunk_dot(blocks, basis, start, width, after, upper):
    if after:
        blocks = [gate(blocks[0], *after)] + blocks[1:]
    part = jnp.dot(
        jnp.concatenate(blocks, axis=0),
        basis[:, start : start + width],
        preferred_element_type=F32,
    )
    return halves(part.astype(BF16), upper)


def lambda_product(place, own, sib, parts, unit, start, width, whole, so_far=None):
    out_rows, seq_tokens = own.shape
    tile_o = largest_tile(out_rows, 128, 256)
    tile_n = min(512, width)
    at_block = start // width
    count = len(parts)
    given = [] if so_far is None else [so_far]

    def kernel(place_ref, own_ref, sib_ref, *rest):
        part_refs, out_ref, acts = rest[:count], rest[-2], rest[-1]

        @pl.when(pl.program_id(0) == 0)
        def _():
            at = 0
            for part in part_refs:
                for h in range(part.shape[0] // unit):
                    rows = pl.ds(pl.multiple_of(place_ref[at] * unit, unit), unit)
                    acts[rows, :] = part[h * unit : (h + 1) * unit, :]
                    at += 1

        for n in range(0, width, tile_n):
            cols = pl.ds(n, min(tile_n, width - n))
            first = jnp.dot(own_ref[...], acts[:seq_tokens, cols], preferred_element_type=F32)
            second = jnp.dot(sib_ref[...], acts[seq_tokens:, cols], preferred_element_type=F32)
            mean = (first * first + second * second) * (1.0 / SEQS)
            out_ref[:, cols] = mean.astype(BF16)

    return pl.pallas_call(
        kernel,
        grid_spec=pltpu.PrefetchScalarGridSpec(
            num_scalar_prefetch=1,
            grid=(out_rows // tile_o,),
            in_specs=[pl.BlockSpec((tile_o, seq_tokens), lambda o, s: (o, 0))] * 2
            + [IN_VMEM] * count
            + [ANYWHERE] * len(given),
            out_specs=pl.BlockSpec((tile_o, width), lambda o, s: (o, at_block)),
            scratch_shapes=[pltpu.VMEM((SEQS * seq_tokens, width), BF16)],
        ),
        out_shape=jax.ShapeDtypeStruct((out_rows, whole), BF16),
        input_output_aliases={3 + count: 0} if given else {},
        compiler_params=vmem(12),
        cost_estimate=pl.CostEstimate(
            flops=2 * out_rows * width * SEQS * seq_tokens,
            bytes_accessed=2 * out_rows * width,
            transcendentals=0,
        ),
        name="lambda_product",
    )(place, own, sib, *parts, *given)


def chip_ring(chips):
    order = list(range(1, chips, 2))
    order = [0] + order + [c for c in range(chips - 1, 0, -1) if c % 2 == 0]
    return {order[i]: order[(i + 1) % chips] for i in range(chips)}


def on_both_cores(pairs):
    return [(CORES * a + k, CORES * b + k) for a, b in pairs for k in range(CORES)]


def powers(n):
    return [1 << b for b in range(n.bit_length() - 1)]


def halves(x, upper):
    half = x.shape[0] // 2
    low, high = x[:half], x[half:]
    return jnp.where(upper, high, low), jnp.where(upper, low, high)


def joined(mine, theirs, upper):
    return jnp.where(
        upper,
        jnp.concatenate([theirs, mine], axis=0),
        jnp.concatenate([mine, theirs], axis=0),
    )


def local(rows_n, cols_n, activations, act_basis, out_grads, grad_basis):
    chips = cols_n // CORES
    col = lax.axis_index("col")
    row = lax.axis_index("row")
    core = col & 1
    swap = lambda x: lax.ppermute(x, "col", [(c, c ^ 1) for c in range(cols_n)])
    trade = lambda x, bit: lax.ppermute(x, "row", [(r, r ^ bit) for r in range(rows_n)])
    bits = powers(rows_n)

    succ = chip_ring(chips)
    pred = {b: a for a, b in succ.items()}
    ring = on_both_cores(sorted(succ.items()))
    blocks = [activations]
    pairs = [(activations, swap(activations))]
    grads = copy_gate(out_grads, pairs[0][1])
    pieces = [grads] + [trade(grads, mask) for mask in range(1, rows_n)]
    for bit in bits:
        pieces = [
            joined(low, high, (row & bit) != 0)
            for low, high in zip(pieces[::2], pieces[1::2])
        ]
    grads = pieces[0]
    for s in range(1, chips):
        block = lax.ppermute(blocks[-1], "col", ring)
        if s == 1:
            block = gate(block, grads)
        blocks.append(block)
        pairs.append((block, swap(block)))

    chip_bits = powers(chips)
    chip_trade = lambda x, bit: lax.ppermute(
        x, "col", on_both_cores([(c, c ^ bit) for c in range(chips)])
    )
    upper_chip = (col & CORES) != 0
    plus = lambda a, b: (a.astype(F32) + b.astype(F32)).astype(BF16)

    def plus_others(x, got, others):
        x = plus(x, got)
        for bit in others[1:]:
            x = plus(x, trade(x, bit))
        return x

    half = chips // 2
    width = act_basis.shape[1]
    (start_l, wide_l), (start_r, wide_r) = column_parts(width)
    early = [b for p in pairs[:half] for b in p]
    late = [b for p in pairs[half:] for b in p]

    part = lax.dot_general(
        grad_basis,
        grads,
        (((0,), (1,)), ((), ())),
        preferred_element_type=F32,
    )
    seq_tokens = part.shape[1] // SEQS
    seqs = [part[:, :seq_tokens], part[:, seq_tokens:]]
    mine = jnp.where(core == 0, seqs[0], seqs[1])
    theirs = jnp.where(core == 0, seqs[1], seqs[0]).astype(BF16)
    mine = mine + swap(theirs).astype(F32)
    mine, away = halves(mine, upper_chip)

    early_bit, early_bits = bits[-1], bits[:-1]
    late_bit, late_bits = bits[0], bits[1:]
    early_upper, late_upper = (row & early_bit) != 0, (row & late_bit) != 0
    keep_l, send_l = chunk_dot(early, act_basis, start_l, wide_l, [theirs], early_upper)
    got_l = trade(send_l, early_bit)
    keep_r, send_r = chunk_dot(
        early, act_basis, start_r, wide_r, [blocks[half], send_l], early_upper
    )

    keep_l = plus(keep_l, got_l)
    send_r, keep_l, away = gates([send_r, keep_l, away.astype(BF16)])
    got_r = trade(send_r, early_bit)
    got_l = trade(keep_l, early_bits[0])
    got_away = chip_trade(away, 1)
    late_l, send_l = chunk_dot(late, act_basis, start_l, wide_l, [send_r], late_upper)

    got_r, got_l, got_away = gates([got_r, got_l, got_away], send_l)
    mine = mine + got_away.astype(F32)
    early_l = plus_others(keep_l, got_l, early_bits)
    keep_r = plus(keep_r, got_r)
    send_l, early_l, keep_r, away = gates([send_l, early_l, keep_r, mine.astype(BF16)])
    got_l = trade(send_l, late_bit)
    got_r = trade(keep_r, early_bits[0])
    early_other_l = trade(early_l, early_bit)
    for bit in chip_bits[1:]:
        mine = mine + chip_trade(away, bit).astype(F32)
        away = mine.astype(BF16)
    late_r, send_r = chunk_dot(late, act_basis, start_r, wide_r, [send_l], late_upper)

    got_r, got_l = gates([got_r, got_l], send_r, early_other_l)
    early_r = plus_others(keep_r, got_r, early_bits)
    send_r, late_l, early_r = gates([send_r, plus(late_l, got_l), early_r])
    got_r = trade(send_r, late_bit)
    got_l = trade(late_l, late_bits[0])

    late_l = plus_others(late_l, got_l, late_bits)
    late_l, late_r, own = gates([late_l, plus(late_r, got_r), away])
    late_other_l = trade(late_l, late_bit)
    got_r = trade(late_r, late_bits[0])
    other_own = chip_trade(own, 1)

    late_r = plus_others(late_r, got_r, late_bits)
    own = joined(own, other_own, upper_chip)
    late_r, early_r, own = gates([late_r, early_r, own], late_other_l)
    late_other_r = trade(late_r, late_bit)
    early_other_r = trade(early_r, early_bit)
    sib = swap(own)

    table = []
    for r in range(rows_n):
        for c in range(cols_n):
            here, k = c // CORES, c % CORES
            place = []
            for _ in range(chips):
                block = (here + k * (chips // SEQS)) % chips
                place += [CORES * block + k, CORES * block + 1 - k]
                here = pred[here]
            flat = []
            for at, bit in ((0, early_bit), (chips, late_bit)):
                low, high = place[at : at + half], place[at + half : at + chips]
                flat += high + low if r & bit else low + high
            table.append(flat)
    place = jnp.asarray(np.array(table, np.int32))
    place = lax.dynamic_index_in_dim(place, row * cols_n + col, 0, keepdims=False)
    unit = activations.shape[0]
    parts_l = [early_l, early_other_l, late_l, late_other_l]
    out = lambda_product(place, own, sib, parts_l, unit, start_l, wide_l, width)
    parts_r = [early_r, early_other_r, late_r, late_other_r]
    return lambda_product(place, own, sib, parts_r, unit, start_r, wide_r, width, out)


def solution(mesh):
    rows_n, cols_n = mesh.shape["row"], mesh.shape["col"]

    def body(activations, act_basis, out_grads, grad_basis):
        return local(rows_n, cols_n, activations, act_basis, out_grads, grad_basis)

    return jax.shard_map(
        body,
        mesh=mesh,
        in_specs=(P("col", "row"), P("row", "col"), P("row", "col"), P("col", "row")),
        out_specs=P("row", "col"),
        check_vma=False,
    )
```

```python
import functools

import jax
import jax.numpy as jnp
import numpy as np
from jax import lax
from jax.experimental import pallas as pl
from jax.experimental.pallas import tpu as pltpu
from jax.sharding import PartitionSpec as P

SEQS = 2
CORES = 2
F32 = jnp.float32
BF16 = jnp.bfloat16
ANYWHERE = pl.BlockSpec(memory_space=pl.ANY)
IN_VMEM = pl.BlockSpec(memory_space=pltpu.VMEM)


def vmem(mib):
    return pltpu.CompilerParams(vmem_limit_bytes=mib * 2**20)


def largest_tile(size, unit, most):
    tile = unit
    for candidate in range(unit, most + 1, unit):
        if size % candidate == 0:
            tile = candidate
    return tile if size % tile == 0 else size


def column_parts(width):
    right = width // 2 if width % 512 == 0 else 128
    return [(0, width - right), (width - right, right)]


def column_tile(start, width, most=256):
    for tile in (512, 256, 128):
        if tile <= most and start % tile == 0 and width % tile == 0:
            return tile
    raise ValueError("columns")


NO_COST = pl.CostEstimate(flops=0, bytes_accessed=0, transcendentals=0)


def gates(arrays, *after):
    count = len(arrays)
    return pl.pallas_call(
        lambda *refs: None,
        in_specs=[ANYWHERE] * (count + len(after)),
        out_specs=[ANYWHERE] * count,
        out_shape=[jax.ShapeDtypeStruct(x.shape, x.dtype) for x in arrays],
        input_output_aliases={i: i for i in range(count)},
        compiler_params=vmem(1),
        cost_estimate=NO_COST,
        name="gates",
    )(*arrays, *after)


def gate(x, *after):
    return gates([x], *after)[0]


def copy_gate(x, after):
    def kernel(x_ref, after_ref, out_ref):
        out_ref[...] = x_ref[...]

    return pl.pallas_call(
        kernel,
        in_specs=[pl.BlockSpec(memory_space=pltpu.VMEM), ANYWHERE],
        out_specs=pl.BlockSpec(memory_space=pltpu.VMEM),
        out_shape=jax.ShapeDtypeStruct(x.shape, x.dtype),
        compiler_params=vmem(2),
        cost_estimate=NO_COST,
        name="copy_gate",
    )(x, after)


def chunk_dot(blocks, basis, start, width, after, upper):
    rows, depth = blocks[0].shape
    tokens = rows * len(blocks)
    tile = column_tile(start, width)
    first = start // tile
    count = len(blocks)

    def kernel(upper_ref, *rest):
        block_refs, basis_ref = rest[:count], rest[count]
        keep_ref, send_ref, joint = rest[-3:]

        @pl.when(pl.program_id(0) == 0)
        def _():
            for i, block_ref in enumerate(block_refs):
                joint[i * rows : (i + 1) * rows, :] = block_ref[...]

        total = jnp.dot(joint[...], basis_ref[...], preferred_element_type=F32)
        total = total.astype(BF16)
        half = tokens // 2
        is_upper = upper_ref[0] != 0
        keep_ref[...] = jnp.where(is_upper, total[half:], total[:half])
        send_ref[...] = jnp.where(is_upper, total[:half], total[half:])

    out_rows = tokens // 2
    return pl.pallas_call(
        kernel,
        grid_spec=pltpu.PrefetchScalarGridSpec(
            num_scalar_prefetch=1,
            grid=(width // tile,),
            in_specs=[IN_VMEM] * count
            + [pl.BlockSpec((depth, tile), lambda n, s: (0, first + n))]
            + [ANYWHERE] * len(after),
            out_specs=[pl.BlockSpec((out_rows, tile), lambda n, s: (0, n))] * 2,
            scratch_shapes=[pltpu.VMEM((tokens, depth), BF16)],
        ),
        out_shape=[jax.ShapeDtypeStruct((out_rows, width), BF16)] * 2,
        compiler_params=vmem(16),
        cost_estimate=pl.CostEstimate(
            flops=2 * tokens * depth * width,
            bytes_accessed=2 * depth * width,
            transcendentals=0,
        ),
        name="chunk_dot",
    )(jnp.reshape(upper, (1,)), *blocks, basis, *after)


def first_chunk_dot(blocks, basis, start, width, after, upper):
    part = jnp.dot(
        gate(jnp.concatenate(blocks, axis=0), *after),
        basis[:, start : start + width],
        preferred_element_type=F32,
    )
    return halves(part.astype(BF16), upper != 0)


def lambda_product(place, own, sib, parts, unit, start, width, whole, so_far=None):
    out_rows, seq_tokens = own.shape
    tile_o = largest_tile(out_rows, 128, 256)
    tile_n = min(512, width)
    at_block = start // width
    count = len(parts)
    given = [] if so_far is None else [so_far]

    def kernel(place_ref, own_ref, sib_ref, *rest):
        part_refs, out_ref, acts = rest[:count], rest[-2], rest[-1]

        @pl.when(pl.program_id(0) == 0)
        def _():
            at = 0
            for part in part_refs:
                for h in range(part.shape[0] // unit):
                    rows = pl.ds(pl.multiple_of(place_ref[at] * unit, unit), unit)
                    acts[rows, :] = part[h * unit : (h + 1) * unit, :]
                    at += 1

        for n in range(0, width, tile_n):
            cols = pl.ds(n, min(tile_n, width - n))
            first = jnp.dot(own_ref[...], acts[:seq_tokens, cols], preferred_element_type=F32)
            second = jnp.dot(sib_ref[...], acts[seq_tokens:, cols], preferred_element_type=F32)
            mean = (first * first + second * second) * (1.0 / SEQS)
            out_ref[:, cols] = mean.astype(BF16)

    return pl.pallas_call(
        kernel,
        grid_spec=pltpu.PrefetchScalarGridSpec(
            num_scalar_prefetch=1,
            grid=(out_rows // tile_o,),
            in_specs=[pl.BlockSpec((tile_o, seq_tokens), lambda o, s: (o, 0))] * 2
            + [IN_VMEM] * count
            + [ANYWHERE] * len(given),
            out_specs=pl.BlockSpec((tile_o, width), lambda o, s: (o, at_block)),
            scratch_shapes=[pltpu.VMEM((SEQS * seq_tokens, width), BF16)],
        ),
        out_shape=jax.ShapeDtypeStruct((out_rows, whole), BF16),
        input_output_aliases={3 + count: 0} if given else {},
        compiler_params=vmem(12),
        cost_estimate=pl.CostEstimate(
            flops=2 * out_rows * width * SEQS * seq_tokens,
            bytes_accessed=2 * out_rows * width,
            transcendentals=0,
        ),
        name="lambda_product",
    )(place, own, sib, *parts, *given)


def chip_ring(chips):
    order = list(range(1, chips, 2))
    order = [0] + order + [c for c in range(chips - 1, 0, -1) if c % 2 == 0]
    return {order[i]: order[(i + 1) % chips] for i in range(chips)}


def on_both_cores(pairs):
    return [(CORES * a + k, CORES * b + k) for a, b in pairs for k in range(CORES)]


def powers(n):
    return [1 << b for b in range(n.bit_length() - 1)]


def halves(x, upper):
    half = x.shape[0] // 2
    low, high = x[:half], x[half:]
    return jnp.where(upper, high, low), jnp.where(upper, low, high)


def joined(mine, theirs, upper):
    return jnp.where(
        upper,
        jnp.concatenate([theirs, mine], axis=0),
        jnp.concatenate([mine, theirs], axis=0),
    )


def local(rows_n, cols_n, activations, act_basis, out_grads, grad_basis):
    chips = cols_n // CORES
    col = lax.axis_index("col")
    row = lax.axis_index("row")
    core = col & 1
    swap = lambda x: lax.ppermute(x, "col", [(c, c ^ 1) for c in range(cols_n)])
    trade = lambda x, bit: lax.ppermute(x, "row", [(r, r ^ bit) for r in range(rows_n)])
    bits = powers(rows_n)

    succ = chip_ring(chips)
    pred = {b: a for a, b in succ.items()}
    ring = on_both_cores(sorted(succ.items()))
    blocks = [activations]
    pairs = [(activations, swap(activations))]
    grads = copy_gate(out_grads, pairs[0][1])
    pieces = [grads] + [trade(grads, mask) for mask in range(1, rows_n)]
    for bit in bits:
        pieces = [
            joined(low, high, (row & bit) != 0)
            for low, high in zip(pieces[::2], pieces[1::2])
        ]
    grads = pieces[0]
    for s in range(1, chips):
        block = lax.ppermute(blocks[-1], "col", ring)
        if s == 1:
            block = gate(block, grads)
        blocks.append(block)
        pairs.append((block, swap(block)))

    chip_bits = powers(chips)
    chip_trade = lambda x, bit: lax.ppermute(
        x, "col", on_both_cores([(c, c ^ bit) for c in range(chips)])
    )
    upper_chip = (col & CORES) != 0
    plus = lambda a, b: (a.astype(F32) + b.astype(F32)).astype(BF16)

    def plus_others(x, got, others):
        x = plus(x, got)
        for bit in others[1:]:
            x = plus(x, trade(x, bit))
        return x

    half = chips // 2
    width = act_basis.shape[1]
    (start_l, wide_l), (start_r, wide_r) = column_parts(width)
    early = [b for p in pairs[:half] for b in p]
    late = [b for p in pairs[half:] for b in p]

    part = lax.dot_general(
        grad_basis,
        grads,
        (((0,), (1,)), ((), ())),
        preferred_element_type=F32,
    )
    seq_tokens = part.shape[1] // SEQS
    seqs = [part[:, :seq_tokens], part[:, seq_tokens:]]
    mine = jnp.where(core == 0, seqs[0], seqs[1])
    theirs = jnp.where(core == 0, seqs[1], seqs[0]).astype(BF16)
    mine = mine + swap(theirs).astype(F32)
    mine, away = halves(mine, upper_chip)

    early_bit, early_bits = bits[-1], bits[:-1]
    late_bit, late_bits = bits[0], bits[1:]
    early_upper, late_upper = row & early_bit, row & late_bit
    keep_l, send_l = first_chunk_dot(
        early, act_basis, start_l, wide_l, [theirs], early_upper
    )
    got_l = trade(send_l, early_bit)
    keep_r, send_r = chunk_dot(
        early, act_basis, start_r, wide_r, [blocks[half], send_l], early_upper
    )

    keep_l = plus(keep_l, got_l)
    send_r, keep_l, away = gates([send_r, keep_l, away.astype(BF16)])
    got_r = trade(send_r, early_bit)
    got_l = trade(keep_l, early_bits[0])
    got_away = chip_trade(away, 1)
    late_l, send_l = chunk_dot(late, act_basis, start_l, wide_l, [send_r], late_upper)

    got_r, got_l, got_away = gates([got_r, got_l, got_away], send_l)
    mine = mine + got_away.astype(F32)
    early_l = plus_others(keep_l, got_l, early_bits)
    keep_r = plus(keep_r, got_r)
    send_l, early_l, keep_r, away = gates([send_l, early_l, keep_r, mine.astype(BF16)])
    got_l = trade(send_l, late_bit)
    got_r = trade(keep_r, early_bits[0])
    early_other_l = trade(early_l, early_bit)
    for bit in chip_bits[1:]:
        mine = mine + chip_trade(away, bit).astype(F32)
        away = mine.astype(BF16)
    late_r, send_r = chunk_dot(late, act_basis, start_r, wide_r, [send_l], late_upper)

    got_r, got_l = gates([got_r, got_l], send_r, early_other_l)
    early_r = plus_others(keep_r, got_r, early_bits)
    send_r, late_l, early_r = gates([send_r, plus(late_l, got_l), early_r])
    got_r = trade(send_r, late_bit)
    got_l = trade(late_l, late_bits[0])

    late_l = plus_others(late_l, got_l, late_bits)
    late_l, late_r, own = gates([late_l, plus(late_r, got_r), away])
    late_other_l = trade(late_l, late_bit)
    got_r = trade(late_r, late_bits[0])
    other_own = chip_trade(own, 1)

    late_r = plus_others(late_r, got_r, late_bits)
    own = joined(own, other_own, upper_chip)
    late_r, early_r, own = gates([late_r, early_r, own], late_other_l)
    late_other_r = trade(late_r, late_bit)
    early_other_r = trade(early_r, early_bit)
    sib = swap(own)

    table = []
    for r in range(rows_n):
        for c in range(cols_n):
            here, k = c // CORES, c % CORES
            place = []
            for _ in range(chips):
                block = (here + k * (chips // SEQS)) % chips
                place += [CORES * block + k, CORES * block + 1 - k]
                here = pred[here]
            flat = []
            for at, bit in ((0, early_bit), (chips, late_bit)):
                low, high = place[at : at + half], place[at + half : at + chips]
                flat += high + low if r & bit else low + high
            table.append(flat)
    place = jnp.asarray(np.array(table, np.int32))
    place = lax.dynamic_index_in_dim(place, row * cols_n + col, 0, keepdims=False)
    unit = activations.shape[0]
    parts_l = [early_l, early_other_l, late_l, late_other_l]
    out = lambda_product(place, own, sib, parts_l, unit, start_l, wide_l, width)
    parts_r = [early_r, early_other_r, late_r, late_other_r]
    return lambda_product(place, own, sib, parts_r, unit, start_r, wide_r, width, out)


def solution(mesh):
    rows_n, cols_n = mesh.shape["row"], mesh.shape["col"]

    def body(activations, act_basis, out_grads, grad_basis):
        return local(rows_n, cols_n, activations, act_basis, out_grads, grad_basis)

    return jax.shard_map(
        body,
        mesh=mesh,
        in_specs=(P("col", "row"), P("row", "col"), P("row", "col"), P("col", "row")),
        out_specs=P("row", "col"),
        check_vma=False,
    )
```

```python
import functools

import jax
import jax.numpy as jnp
import numpy as np
from jax import lax
from jax.experimental import pallas as pl
from jax.experimental.pallas import tpu as pltpu
from jax.sharding import PartitionSpec as P

SEQS = 2
CORES = 2
F32 = jnp.float32
BF16 = jnp.bfloat16
ANYWHERE = pl.BlockSpec(memory_space=pl.ANY)
IN_VMEM = pl.BlockSpec(memory_space=pltpu.VMEM)


def vmem(mib):
    return pltpu.CompilerParams(vmem_limit_bytes=mib * 2**20)


def largest_tile(size, unit, most):
    tile = unit
    for candidate in range(unit, most + 1, unit):
        if size % candidate == 0:
            tile = candidate
    return tile if size % tile == 0 else size


def column_parts(width):
    right = width // 2 if width % 512 == 0 else 128
    return [(0, width - right), (width - right, right)]


def column_tile(start, width, most=256):
    for tile in (512, 256, 128):
        if tile <= most and start % tile == 0 and width % tile == 0:
            return tile
    raise ValueError("columns")


NO_COST = pl.CostEstimate(flops=0, bytes_accessed=0, transcendentals=0)


def gates(arrays, *after):
    count = len(arrays)
    return pl.pallas_call(
        lambda *refs: None,
        in_specs=[ANYWHERE] * (count + len(after)),
        out_specs=[ANYWHERE] * count,
        out_shape=[jax.ShapeDtypeStruct(x.shape, x.dtype) for x in arrays],
        input_output_aliases={i: i for i in range(count)},
        compiler_params=vmem(1),
        cost_estimate=NO_COST,
        name="gates",
    )(*arrays, *after)


def gate(x, *after):
    return gates([x], *after)[0]


def copy_gate(x, after):
    def kernel(x_ref, after_ref, out_ref):
        out_ref[...] = x_ref[...]

    return pl.pallas_call(
        kernel,
        in_specs=[pl.BlockSpec(memory_space=pltpu.VMEM), ANYWHERE],
        out_specs=pl.BlockSpec(memory_space=pltpu.VMEM),
        out_shape=jax.ShapeDtypeStruct(x.shape, x.dtype),
        compiler_params=vmem(2),
        cost_estimate=NO_COST,
        name="copy_gate",
    )(x, after)


def chunk_dot(blocks, basis, start, width, after, upper):
    rows, depth = blocks[0].shape
    tokens = rows * len(blocks)
    tile = column_tile(start, width)
    first = start // tile
    count = len(blocks)

    def kernel(upper_ref, *rest):
        block_refs, basis_ref = rest[:count], rest[count]
        keep_ref, send_ref, joint = rest[-3:]

        @pl.when(pl.program_id(0) == 0)
        def _():
            for i, block_ref in enumerate(block_refs):
                joint[i * rows : (i + 1) * rows, :] = block_ref[...]

        total = jnp.dot(joint[...], basis_ref[...], preferred_element_type=F32)
        total = total.astype(BF16)
        half = tokens // 2
        is_upper = upper_ref[0] != 0
        keep_ref[...] = jnp.where(is_upper, total[half:], total[:half])
        send_ref[...] = jnp.where(is_upper, total[:half], total[half:])

    out_rows = tokens // 2
    return pl.pallas_call(
        kernel,
        grid_spec=pltpu.PrefetchScalarGridSpec(
            num_scalar_prefetch=1,
            grid=(width // tile,),
            in_specs=[IN_VMEM] * count
            + [pl.BlockSpec((depth, tile), lambda n, s: (0, first + n))]
            + [ANYWHERE] * len(after),
            out_specs=[pl.BlockSpec((out_rows, tile), lambda n, s: (0, n))] * 2,
            scratch_shapes=[pltpu.VMEM((tokens, depth), BF16)],
        ),
        out_shape=[jax.ShapeDtypeStruct((out_rows, width), BF16)] * 2,
        compiler_params=vmem(16),
        cost_estimate=pl.CostEstimate(
            flops=2 * tokens * depth * width,
            bytes_accessed=2 * depth * width,
            transcendentals=0,
        ),
        name="chunk_dot",
    )(jnp.reshape(upper, (1,)), *blocks, basis, *after)


def lambda_product(place, own, sib, parts, unit, start, width, whole, so_far=None):
    out_rows, seq_tokens = own.shape
    tile_o = largest_tile(out_rows, 128, 256)
    tile_n = min(512, width)
    at_block = start // width
    count = len(parts)
    given = [] if so_far is None else [so_far]

    def kernel(place_ref, own_ref, sib_ref, *rest):
        part_refs, out_ref, acts, sems = rest[:count], rest[-3], rest[-2], rest[-1]

        @pl.when(pl.program_id(0) == 0)
        def _():
            copies = []
            for part in part_refs:
                for h in range(part.shape[0] // unit):
                    at = len(copies)
                    rows = pl.ds(pl.multiple_of(place_ref[at] * unit, unit), unit)
                    copies.append(
                        pltpu.make_async_copy(
                            part.at[pl.ds(h * unit, unit), :], acts.at[rows, :], sems.at[at]
                        )
                    )
            for copy in copies:
                copy.start()
            for copy in copies:
                copy.wait()

        for n in range(0, width, tile_n):
            cols = pl.ds(n, min(tile_n, width - n))
            first = jnp.dot(own_ref[...], acts[:seq_tokens, cols], preferred_element_type=F32)
            second = jnp.dot(sib_ref[...], acts[seq_tokens:, cols], preferred_element_type=F32)
            mean = (first * first + second * second) * (1.0 / SEQS)
            out_ref[:, cols] = mean.astype(BF16)

    return pl.pallas_call(
        kernel,
        grid_spec=pltpu.PrefetchScalarGridSpec(
            num_scalar_prefetch=1,
            grid=(out_rows // tile_o,),
            in_specs=[pl.BlockSpec((tile_o, seq_tokens), lambda o, s: (o, 0))] * 2
            + [ANYWHERE] * (count + len(given)),
            out_specs=pl.BlockSpec((tile_o, width), lambda o, s: (o, at_block)),
            scratch_shapes=[
                pltpu.VMEM((SEQS * seq_tokens, width), BF16),
                pltpu.SemaphoreType.DMA((SEQS * seq_tokens // unit,)),
            ],
        ),
        out_shape=jax.ShapeDtypeStruct((out_rows, whole), BF16),
        input_output_aliases={3 + count: 0} if given else {},
        compiler_params=vmem(12),
        cost_estimate=pl.CostEstimate(
            flops=2 * out_rows * width * SEQS * seq_tokens,
            bytes_accessed=2 * out_rows * width,
            transcendentals=0,
        ),
        name="lambda_product",
    )(place, own, sib, *parts, *given)


def chip_ring(chips):
    order = list(range(1, chips, 2))
    order = [0] + order + [c for c in range(chips - 1, 0, -1) if c % 2 == 0]
    return {order[i]: order[(i + 1) % chips] for i in range(chips)}


def on_both_cores(pairs):
    return [(CORES * a + k, CORES * b + k) for a, b in pairs for k in range(CORES)]


def powers(n):
    return [1 << b for b in range(n.bit_length() - 1)]


def halves(x, upper):
    half = x.shape[0] // 2
    low, high = x[:half], x[half:]
    return jnp.where(upper, high, low), jnp.where(upper, low, high)


def joined(mine, theirs, upper):
    return jnp.where(
        upper,
        jnp.concatenate([theirs, mine], axis=0),
        jnp.concatenate([mine, theirs], axis=0),
    )


def local(rows_n, cols_n, activations, act_basis, out_grads, grad_basis):
    chips = cols_n // CORES
    col = lax.axis_index("col")
    row = lax.axis_index("row")
    core = col & 1
    swap = lambda x: lax.ppermute(x, "col", [(c, c ^ 1) for c in range(cols_n)])
    trade = lambda x, bit: lax.ppermute(x, "row", [(r, r ^ bit) for r in range(rows_n)])
    bits = powers(rows_n)

    succ = chip_ring(chips)
    pred = {b: a for a, b in succ.items()}
    ring = on_both_cores(sorted(succ.items()))
    blocks = [activations]
    pairs = [(activations, swap(activations))]
    grads = copy_gate(out_grads, pairs[0][1])
    pieces = [grads] + [trade(grads, mask) for mask in range(1, rows_n)]
    for bit in bits:
        pieces = [
            joined(low, high, (row & bit) != 0)
            for low, high in zip(pieces[::2], pieces[1::2])
        ]
    grads = pieces[0]
    chip_bits = powers(chips)
    chip_trade = lambda x, bit: lax.ppermute(
        x, "col", on_both_cores([(c, c ^ bit) for c in range(chips)])
    )
    upper_chip = (col & CORES) != 0
    plus = lambda a, b: (a.astype(F32) + b.astype(F32)).astype(BF16)

    def plus_others(x, got, others):
        x = plus(x, got)
        for bit in others[1:]:
            x = plus(x, trade(x, bit))
        return x

    part = lax.dot_general(
        grad_basis,
        grads,
        (((0,), (1,)), ((), ())),
        preferred_element_type=F32,
    )
    seq_tokens = part.shape[1] // SEQS
    seqs = [part[:, :seq_tokens], part[:, seq_tokens:]]
    mine = jnp.where(core == 0, seqs[0], seqs[1])
    theirs = jnp.where(core == 0, seqs[1], seqs[0]).astype(BF16)
    mine = mine + swap(theirs).astype(F32)
    mine, away = halves(mine, upper_chip)

    def ring_step(after):
        blocks.append(gate(lax.ppermute(blocks[-1], "col", ring), after))
        pairs.append((blocks[-1], swap(blocks[-1])))

    ring_step(grads)

    width = act_basis.shape[1]
    (start_l, wide_l), (start_r, wide_r) = column_parts(width)
    chunks = [[0], list(range(1, chips - 1)), [chips - 1]]
    def product(n, columns, after, upper):
        tokens = [b for s in chunks[n] for b in pairs[s]]
        return chunk_dot(tokens, act_basis, *columns, after, upper)

    left = functools.partial(product, columns=(start_l, wide_l))
    right = functools.partial(product, columns=(start_r, wide_r))

    early_bit, early_bits = bits[-1], bits[:-1]
    late_bit, late_bits = bits[0], bits[1:]
    early_upper, late_upper = row & early_bit, row & late_bit

    keep_l, send_l = left(0, after=[blocks[1]], upper=early_upper)
    got_l = trade(send_l, early_bit)
    keep_r, send_r = right(0, after=[send_l], upper=early_upper)
    send_r, keep_l = gates([send_r, plus(keep_l, got_l)])
    got_r = trade(send_r, early_bit)
    got_l = trade(keep_l, early_bits[0])
    ring_step(send_r)
    for _ in range(3, chips):
        blocks.append(lax.ppermute(blocks[-1], "col", ring))
        pairs.append((blocks[-1], swap(blocks[-1])))
    mid_l, send_l = left(1, after=[send_r], upper=early_upper)

    got_r, got_l = gates([got_r, got_l], send_l)
    first_l = plus_others(keep_l, got_l, early_bits)
    send_l, first_l, keep_r = gates([send_l, first_l, plus(keep_r, got_r)])
    got_l = trade(send_l, early_bit)
    first_other_l = trade(first_l, early_bit)
    got_r = trade(keep_r, early_bits[0])
    mid_r, send_r = right(1, after=[send_l], upper=early_upper)

    got_l, got_r, first_other_l = gates([got_l, got_r, first_other_l], send_r)
    first_r = plus_others(keep_r, got_r, early_bits)
    send_r, mid_l, away = gates([send_r, plus(mid_l, got_l), away.astype(BF16)])
    got_r = trade(send_r, early_bit)
    got_l = trade(mid_l, early_bits[0])
    got_away = chip_trade(away, 1)
    last_l, send_l = left(2, after=[send_r], upper=late_upper)

    got_r, got_l, got_away = gates([got_r, got_l, got_away], send_l)
    mine = mine + got_away.astype(F32)
    mid_l = plus_others(mid_l, got_l, early_bits)
    mid_r = plus(mid_r, got_r)
    send_l, mid_l, mid_r, away = gates([send_l, mid_l, mid_r, mine.astype(BF16)])
    got_l = trade(send_l, late_bit)
    got_r = trade(mid_r, early_bits[0])
    mid_other_l = trade(mid_l, early_bit)
    for bit in chip_bits[1:]:
        mine = mine + chip_trade(away, bit).astype(F32)
        away = mine.astype(BF16)
    last_r, send_r = right(2, after=[send_l], upper=late_upper)

    got_r, got_l = gates([got_r, got_l], send_r, mid_other_l)
    mid_r = plus_others(mid_r, got_r, early_bits)
    send_r, last_l, mid_r = gates([send_r, plus(last_l, got_l), mid_r])
    got_r = trade(send_r, late_bit)
    got_l = trade(last_l, late_bits[0])

    last_l = plus_others(last_l, got_l, late_bits)
    last_l, last_r, own = gates([last_l, plus(last_r, got_r), away])
    last_other_l = trade(last_l, late_bit)
    got_r = trade(last_r, late_bits[0])
    other_own = chip_trade(own, 1)

    last_r = plus_others(last_r, got_r, late_bits)
    own = joined(own, other_own, upper_chip)
    last_r, mid_r, first_r, own = gates([last_r, mid_r, first_r, own], last_other_l)
    last_other_r = trade(last_r, late_bit)
    first_other_r = trade(first_r, early_bit)
    mid_other_r = trade(mid_r, early_bit)
    sib = swap(own)

    table = []
    for r in range(rows_n):
        for c in range(cols_n):
            here, k = c // CORES, c % CORES
            place = []
            for _ in range(chips):
                block = (here + k * (chips // SEQS)) % chips
                place += [CORES * block + k, CORES * block + 1 - k]
                here = pred[here]
            flat = []
            for chunk, bit in zip(chunks, (early_bit, early_bit, late_bit)):
                units = place[CORES * chunk[0] : CORES * (chunk[-1] + 1)]
                low, high = units[: len(units) // 2], units[len(units) // 2 :]
                flat += high + low if r & bit else low + high
            table.append(flat)
    place = jnp.asarray(np.array(table, np.int32))
    place = lax.dynamic_index_in_dim(place, row * cols_n + col, 0, keepdims=False)
    unit = activations.shape[0]
    parts_l = [first_l, first_other_l, mid_l, mid_other_l, last_l, last_other_l]
    out = lambda_product(place, own, sib, parts_l, unit, start_l, wide_l, width)
    parts_r = [first_r, first_other_r, mid_r, mid_other_r, last_r, last_other_r]
    return lambda_product(place, own, sib, parts_r, unit, start_r, wide_r, width, out)


def solution(mesh):
    rows_n, cols_n = mesh.shape["row"], mesh.shape["col"]

    def body(activations, act_basis, out_grads, grad_basis):
        return local(rows_n, cols_n, activations, act_basis, out_grads, grad_basis)

    return jax.shard_map(
        body,
        mesh=mesh,
        in_specs=(P("col", "row"), P("row", "col"), P("row", "col"), P("col", "row")),
        out_specs=P("row", "col"),
        check_vma=False,
    )
```

```python
import functools

import jax
import jax.numpy as jnp
import numpy as np
from jax import lax
from jax.experimental import pallas as pl
from jax.experimental.pallas import tpu as pltpu
from jax.sharding import PartitionSpec as P

SEQS = 2
CORES = 2
F32 = jnp.float32
BF16 = jnp.bfloat16
ANYWHERE = pl.BlockSpec(memory_space=pl.ANY)
IN_VMEM = pl.BlockSpec(memory_space=pltpu.VMEM)


def vmem(mib):
    return pltpu.CompilerParams(vmem_limit_bytes=mib * 2**20)


def largest_tile(size, unit, most):
    tile = unit
    for candidate in range(unit, most + 1, unit):
        if size % candidate == 0:
            tile = candidate
    return tile if size % tile == 0 else size


def column_parts(width):
    right = width // 2 if width % 512 == 0 else 128
    return [(0, width - right), (width - right, right)]


def column_tile(start, width, most=256):
    for tile in (512, 256, 128):
        if tile <= most and start % tile == 0 and width % tile == 0:
            return tile
    raise ValueError("columns")


NO_COST = pl.CostEstimate(flops=0, bytes_accessed=0, transcendentals=0)


def gates(arrays, *after):
    count = len(arrays)
    return pl.pallas_call(
        lambda *refs: None,
        in_specs=[ANYWHERE] * (count + len(after)),
        out_specs=[ANYWHERE] * count,
        out_shape=[jax.ShapeDtypeStruct(x.shape, x.dtype) for x in arrays],
        input_output_aliases={i: i for i in range(count)},
        compiler_params=vmem(1),
        cost_estimate=NO_COST,
        name="gates",
    )(*arrays, *after)


def gate(x, *after):
    return gates([x], *after)[0]


def copy_gate(x, after):
    def kernel(x_ref, after_ref, out_ref):
        out_ref[...] = x_ref[...]

    return pl.pallas_call(
        kernel,
        in_specs=[pl.BlockSpec(memory_space=pltpu.VMEM), ANYWHERE],
        out_specs=pl.BlockSpec(memory_space=pltpu.VMEM),
        out_shape=jax.ShapeDtypeStruct(x.shape, x.dtype),
        compiler_params=vmem(2),
        cost_estimate=NO_COST,
        name="copy_gate",
    )(x, after)


def chunk_dot(blocks, basis, start, width, after, upper):
    rows, depth = blocks[0].shape
    tokens = rows * len(blocks)
    tile = column_tile(start, width)
    first = start // tile
    count = len(blocks)

    def kernel(upper_ref, *rest):
        block_refs, basis_ref = rest[:count], rest[count]
        keep_ref, send_ref, joint = rest[-3:]

        @pl.when(pl.program_id(0) == 0)
        def _():
            for i, block_ref in enumerate(block_refs):
                joint[i * rows : (i + 1) * rows, :] = block_ref[...]

        total = jnp.dot(joint[...], basis_ref[...], preferred_element_type=F32)
        total = total.astype(BF16)
        half = tokens // 2
        is_upper = upper_ref[0] != 0
        keep_ref[...] = jnp.where(is_upper, total[half:], total[:half])
        send_ref[...] = jnp.where(is_upper, total[:half], total[half:])

    out_rows = tokens // 2
    return pl.pallas_call(
        kernel,
        grid_spec=pltpu.PrefetchScalarGridSpec(
            num_scalar_prefetch=1,
            grid=(width // tile,),
            in_specs=[IN_VMEM] * count
            + [pl.BlockSpec((depth, tile), lambda n, s: (0, first + n))]
            + [ANYWHERE] * len(after),
            out_specs=[pl.BlockSpec((out_rows, tile), lambda n, s: (0, n))] * 2,
            scratch_shapes=[pltpu.VMEM((tokens, depth), BF16)],
        ),
        out_shape=[jax.ShapeDtypeStruct((out_rows, width), BF16)] * 2,
        compiler_params=vmem(14),
        cost_estimate=pl.CostEstimate(
            flops=2 * tokens * depth * width,
            bytes_accessed=2 * depth * width,
            transcendentals=0,
        ),
        name="chunk_dot",
    )(jnp.reshape(upper, (1,)), *blocks, basis, *after)


def first_chunk_dot(blocks, basis, start, width, after, upper):
    part = jnp.dot(
        gate(jnp.concatenate(blocks, axis=0), *after),
        basis[:, start : start + width],
        preferred_element_type=F32,
    )
    return halves(part.astype(BF16), upper != 0)


def lambda_product(place, own, sib, parts, unit, start, width, whole, so_far=None):
    out_rows, seq_tokens = own.shape
    tile_o = largest_tile(out_rows, 128, 256)
    tile_n = width // 2 if width % 256 == 0 else width
    at_block = start // width
    count = len(parts)
    given = [] if so_far is None else [so_far]

    def kernel(place_ref, own_ref, sib_ref, *rest):
        part_refs, out_ref, acts = rest[:count], rest[-2], rest[-1]

        @pl.when(pl.program_id(0) == 0)
        def _():
            at = 0
            for part in part_refs:
                for h in range(part.shape[0] // unit):
                    rows = pl.ds(pl.multiple_of(place_ref[at] * unit, unit), unit)
                    acts[rows, :] = part[h * unit : (h + 1) * unit, :]
                    at += 1

        for n in range(0, width, tile_n):
            cols = pl.ds(n, min(tile_n, width - n))
            first = jnp.dot(own_ref[...], acts[:seq_tokens, cols], preferred_element_type=F32)
            second = jnp.dot(sib_ref[...], acts[seq_tokens:, cols], preferred_element_type=F32)
            mean = (first * first + second * second) * (1.0 / SEQS)
            out_ref[:, cols] = mean.astype(BF16)

    return pl.pallas_call(
        kernel,
        grid_spec=pltpu.PrefetchScalarGridSpec(
            num_scalar_prefetch=1,
            grid=(out_rows // tile_o,),
            in_specs=[pl.BlockSpec((tile_o, seq_tokens), lambda o, s: (o, 0))] * 2
            + [IN_VMEM] * count
            + [ANYWHERE] * len(given),
            out_specs=pl.BlockSpec((tile_o, width), lambda o, s: (o, at_block)),
            scratch_shapes=[pltpu.VMEM((SEQS * seq_tokens, width), BF16)],
        ),
        out_shape=jax.ShapeDtypeStruct((out_rows, whole), BF16),
        input_output_aliases={3 + count: 0} if given else {},
        compiler_params=vmem(8),
        cost_estimate=pl.CostEstimate(
            flops=2 * out_rows * width * SEQS * seq_tokens,
            bytes_accessed=2 * out_rows * width,
            transcendentals=0,
        ),
        name="lambda_product",
    )(place, own, sib, *parts, *given)


def chip_ring(chips):
    order = list(range(1, chips, 2))
    order = [0] + order + [c for c in range(chips - 1, 0, -1) if c % 2 == 0]
    return {order[i]: order[(i + 1) % chips] for i in range(chips)}


def on_both_cores(pairs):
    return [(CORES * a + k, CORES * b + k) for a, b in pairs for k in range(CORES)]


def powers(n):
    return [1 << b for b in range(n.bit_length() - 1)]


def halves(x, upper):
    half = x.shape[0] // 2
    low, high = x[:half], x[half:]
    return jnp.where(upper, high, low), jnp.where(upper, low, high)


def joined(mine, theirs, upper):
    return jnp.where(
        upper,
        jnp.concatenate([theirs, mine], axis=0),
        jnp.concatenate([mine, theirs], axis=0),
    )


def local(rows_n, cols_n, activations, act_basis, out_grads, grad_basis):
    chips = cols_n // CORES
    col = lax.axis_index("col")
    row = lax.axis_index("row")
    core = col & 1
    swap = lambda x: lax.ppermute(x, "col", [(c, c ^ 1) for c in range(cols_n)])
    trade = lambda x, bit: lax.ppermute(x, "row", [(r, r ^ bit) for r in range(rows_n)])
    bits = powers(rows_n)

    succ = chip_ring(chips)
    pred = {b: a for a, b in succ.items()}
    ring = on_both_cores(sorted(succ.items()))
    blocks = [activations]
    pairs = [(activations, swap(activations))]
    grads = copy_gate(out_grads, pairs[0][1])
    pieces = [grads] + [trade(grads, mask) for mask in range(1, rows_n)]
    for bit in bits:
        pieces = [
            joined(low, high, (row & bit) != 0)
            for low, high in zip(pieces[::2], pieces[1::2])
        ]
    grads = pieces[0]
    for s in range(1, chips):
        block = lax.ppermute(blocks[-1], "col", ring)
        if s == 1:
            block = gate(block, grads)
        blocks.append(block)
        pairs.append((block, swap(block)))

    chip_bits = powers(chips)
    chip_trade = lambda x, bit: lax.ppermute(
        x, "col", on_both_cores([(c, c ^ bit) for c in range(chips)])
    )
    upper_chip = (col & CORES) != 0
    plus = lambda a, b: (a.astype(F32) + b.astype(F32)).astype(BF16)

    def plus_others(x, got, others):
        x = plus(x, got)
        for bit in others[1:]:
            x = plus(x, trade(x, bit))
        return x

    half = chips // 2
    width = act_basis.shape[1]
    (start_l, wide_l), (start_r, wide_r) = column_parts(width)
    early = [b for p in pairs[:half] for b in p]
    late = [b for p in pairs[half:] for b in p]

    part = lax.dot_general(
        grad_basis,
        grads,
        (((0,), (1,)), ((), ())),
        preferred_element_type=F32,
    )
    seq_tokens = part.shape[1] // SEQS
    seqs = [part[:, :seq_tokens], part[:, seq_tokens:]]
    mine = jnp.where(core == 0, seqs[0], seqs[1])
    theirs = jnp.where(core == 0, seqs[1], seqs[0]).astype(BF16)
    mine = mine + swap(theirs).astype(F32)
    mine, away = halves(mine, upper_chip)

    early_bit, early_bits = bits[-1], bits[:-1]
    late_bit, late_bits = bits[0], bits[1:]
    early_upper, late_upper = row & early_bit, row & late_bit
    table = []
    for r in range(rows_n):
        for c in range(cols_n):
            here, k = c // CORES, c % CORES
            place = []
            for _ in range(chips):
                block = (here + k * (chips // SEQS)) % chips
                place += [CORES * block + k, CORES * block + 1 - k]
                here = pred[here]
            flat = []
            for at, bit in ((0, early_bit), (chips, late_bit)):
                low, high = place[at : at + half], place[at + half : at + chips]
                flat += high + low if r & bit else low + high
            table.append(flat)
    place = jnp.asarray(np.array(table, np.int32))
    place = lax.dynamic_index_in_dim(place, row * cols_n + col, 0, keepdims=False)

    keep_l, send_l = first_chunk_dot(
        early, act_basis, start_l, wide_l, [theirs, place], early_upper
    )
    got_l = trade(send_l, early_bit)
    keep_r, send_r = chunk_dot(
        early, act_basis, start_r, wide_r, [blocks[half], send_l], early_upper
    )

    keep_l = plus(keep_l, got_l)
    send_r, keep_l, away = gates([send_r, keep_l, away.astype(BF16)])
    got_r = trade(send_r, early_bit)
    got_l = trade(keep_l, early_bits[0])
    got_away = chip_trade(away, 1)
    late_l, send_l = chunk_dot(late, act_basis, start_l, wide_l, [send_r], late_upper)

    got_r, got_l, got_away = gates([got_r, got_l, got_away], send_l)
    mine = mine + got_away.astype(F32)
    early_l = plus_others(keep_l, got_l, early_bits)
    keep_r = plus(keep_r, got_r)
    send_l, early_l, keep_r, away = gates([send_l, early_l, keep_r, mine.astype(BF16)])
    got_l = trade(send_l, late_bit)
    got_r = trade(keep_r, early_bits[0])
    early_other_l = trade(early_l, early_bit)
    for bit in chip_bits[1:]:
        mine = mine + chip_trade(away, bit).astype(F32)
        away = mine.astype(BF16)
    late_r, send_r = chunk_dot(late, act_basis, start_r, wide_r, [send_l], late_upper)

    got_r, got_l = gates([got_r, got_l], send_r, early_other_l)
    early_r = plus_others(keep_r, got_r, early_bits)
    send_r, late_l, early_r = gates([send_r, plus(late_l, got_l), early_r])
    got_r = trade(send_r, late_bit)
    got_l = trade(late_l, late_bits[0])

    late_l = plus_others(late_l, got_l, late_bits)
    late_l, late_r = gates([late_l, plus(late_r, got_r)])
    late_other_l = trade(late_l, late_bit)
    got_r = trade(late_r, late_bits[0])
    other_own = chip_trade(away, 1)

    late_r = plus_others(late_r, got_r, late_bits)
    own = joined(away, other_own, upper_chip)
    late_r, early_r, own = gates([late_r, early_r, own], late_other_l)
    late_other_r = trade(late_r, late_bit)
    early_other_r = trade(early_r, early_bit)
    sib = swap(own)

    unit = activations.shape[0]
    parts_l = [early_l, early_other_l, late_l, late_other_l]
    out = lambda_product(place, own, sib, parts_l, unit, start_l, wide_l, width)
    parts_r = [early_r, early_other_r, late_r, late_other_r]
    return lambda_product(place, own, sib, parts_r, unit, start_r, wide_r, width, out)


def solution(mesh):
    rows_n, cols_n = mesh.shape["row"], mesh.shape["col"]

    def body(activations, act_basis, out_grads, grad_basis):
        return local(rows_n, cols_n, activations, act_basis, out_grads, grad_basis)

    return jax.shard_map(
        body,
        mesh=mesh,
        in_specs=(P("col", "row"), P("row", "col"), P("row", "col"), P("col", "row")),
        out_specs=P("row", "col"),
        check_vma=False,
    )
```

```python
import functools

import jax
import jax.numpy as jnp
import numpy as np
from jax import lax
from jax.experimental import pallas as pl
from jax.experimental.pallas import tpu as pltpu
from jax.sharding import PartitionSpec as P

SEQS = 2
CORES = 2
F32 = jnp.float32
BF16 = jnp.bfloat16
ANYWHERE = pl.BlockSpec(memory_space=pl.ANY)
IN_VMEM = pl.BlockSpec(memory_space=pltpu.VMEM)


def vmem(mib):
    return pltpu.CompilerParams(vmem_limit_bytes=mib * 2**20)


def largest_tile(size, unit, most):
    tile = unit
    for candidate in range(unit, most + 1, unit):
        if size % candidate == 0:
            tile = candidate
    return tile if size % tile == 0 else size


def column_parts(width):
    right = width // 2 if width % 512 == 0 else 128
    return [(0, width - right), (width - right, right)]


def column_tile(start, width, most=256):
    for tile in (512, 256, 128):
        if tile <= most and start % tile == 0 and width % tile == 0:
            return tile
    raise ValueError("columns")


NO_COST = pl.CostEstimate(flops=0, bytes_accessed=0, transcendentals=0)


def gates(arrays, *after):
    count = len(arrays)
    return pl.pallas_call(
        lambda *refs: None,
        in_specs=[ANYWHERE] * (count + len(after)),
        out_specs=[ANYWHERE] * count,
        out_shape=[jax.ShapeDtypeStruct(x.shape, x.dtype) for x in arrays],
        input_output_aliases={i: i for i in range(count)},
        compiler_params=vmem(1),
        cost_estimate=NO_COST,
        name="gates",
    )(*arrays, *after)


def gate(x, *after):
    return gates([x], *after)[0]


def copy_gate(x, after):
    def kernel(x_ref, after_ref, out_ref):
        out_ref[...] = x_ref[...]

    return pl.pallas_call(
        kernel,
        in_specs=[pl.BlockSpec(memory_space=pltpu.VMEM), ANYWHERE],
        out_specs=pl.BlockSpec(memory_space=pltpu.VMEM),
        out_shape=jax.ShapeDtypeStruct(x.shape, x.dtype),
        compiler_params=vmem(2),
        cost_estimate=NO_COST,
        name="copy_gate",
    )(x, after)


def chunk_dot(blocks, basis, start, width, after, upper):
    rows, depth = blocks[0].shape
    tokens = rows * len(blocks)
    tile = column_tile(start, width)
    first = start // tile
    count = len(blocks)

    def kernel(upper_ref, *rest):
        block_refs, basis_ref = rest[:count], rest[count]
        keep_ref, send_ref, joint = rest[-3:]

        @pl.when(pl.program_id(0) == 0)
        def _():
            for i, block_ref in enumerate(block_refs):
                joint[i * rows : (i + 1) * rows, :] = block_ref[...]

        total = jnp.dot(joint[...], basis_ref[...], preferred_element_type=F32)
        total = total.astype(BF16)
        half = tokens // 2
        is_upper = upper_ref[0] != 0
        keep_ref[...] = jnp.where(is_upper, total[half:], total[:half])
        send_ref[...] = jnp.where(is_upper, total[:half], total[half:])

    out_rows = tokens // 2
    return pl.pallas_call(
        kernel,
        grid_spec=pltpu.PrefetchScalarGridSpec(
            num_scalar_prefetch=1,
            grid=(width // tile,),
            in_specs=[IN_VMEM] * count
            + [pl.BlockSpec((depth, tile), lambda n, s: (0, first + n))]
            + [ANYWHERE] * len(after),
            out_specs=[pl.BlockSpec((out_rows, tile), lambda n, s: (0, n))] * 2,
            scratch_shapes=[pltpu.VMEM((tokens, depth), BF16)],
        ),
        out_shape=[jax.ShapeDtypeStruct((out_rows, width), BF16)] * 2,
        compiler_params=vmem(14),
        cost_estimate=pl.CostEstimate(
            flops=2 * tokens * depth * width,
            bytes_accessed=2 * depth * width,
            transcendentals=0,
        ),
        name="chunk_dot",
    )(jnp.reshape(upper, (1,)), *blocks, basis, *after)


def first_chunk_dot(blocks, basis, start, width, after, upper):
    part = jnp.dot(
        gate(jnp.concatenate(blocks, axis=0), *after),
        basis[:, start : start + width],
        preferred_element_type=F32,
    )
    return halves(part.astype(BF16), upper != 0)


def lambda_product(place, own, sib, parts, unit, start, width, whole, so_far=None):
    out_rows, seq_tokens = own.shape
    tile_o = largest_tile(out_rows, 128, 256)
    tile_n = min(512, width)
    at_block = start // width
    count = len(parts)
    given = [] if so_far is None else [so_far]

    def kernel(place_ref, own_ref, sib_ref, *rest):
        part_refs, out_ref, acts = rest[:count], rest[-2], rest[-1]

        @pl.when(pl.program_id(0) == 0)
        def _():
            at = 0
            for part in part_refs:
                for h in range(part.shape[0] // unit):
                    rows = pl.ds(pl.multiple_of(place_ref[at] * unit, unit), unit)
                    acts[rows, :] = part[h * unit : (h + 1) * unit, :]
                    at += 1

        for n in range(0, width, tile_n):
            cols = pl.ds(n, min(tile_n, width - n))
            first = jnp.dot(own_ref[...], acts[:seq_tokens, cols], preferred_element_type=F32)
            second = jnp.dot(sib_ref[...], acts[seq_tokens:, cols], preferred_element_type=F32)
            mean = (first * first + second * second) * (1.0 / SEQS)
            out_ref[:, cols] = mean.astype(BF16)

    return pl.pallas_call(
        kernel,
        grid_spec=pltpu.PrefetchScalarGridSpec(
            num_scalar_prefetch=1,
            grid=(out_rows // tile_o,),
            in_specs=[pl.BlockSpec((tile_o, seq_tokens), lambda o, s: (o, 0))] * 2
            + [IN_VMEM] * count
            + [ANYWHERE] * len(given),
            out_specs=pl.BlockSpec((tile_o, width), lambda o, s: (o, at_block)),
            scratch_shapes=[pltpu.VMEM((SEQS * seq_tokens, width), BF16)],
        ),
        out_shape=jax.ShapeDtypeStruct((out_rows, whole), BF16),
        input_output_aliases={3 + count: 0} if given else {},
        compiler_params=vmem(8),
        cost_estimate=pl.CostEstimate(
            flops=2 * out_rows * width * SEQS * seq_tokens,
            bytes_accessed=2 * out_rows * width,
            transcendentals=0,
        ),
        name="lambda_product",
    )(place, own, sib, *parts, *given)


def chip_ring(chips):
    order = list(range(1, chips, 2))
    order = [0] + order + [c for c in range(chips - 1, 0, -1) if c % 2 == 0]
    return {order[i]: order[(i + 1) % chips] for i in range(chips)}


def on_both_cores(pairs):
    return [(CORES * a + k, CORES * b + k) for a, b in pairs for k in range(CORES)]


def powers(n):
    return [1 << b for b in range(n.bit_length() - 1)]


def halves(x, upper):
    half = x.shape[0] // 2
    low, high = x[:half], x[half:]
    return jnp.where(upper, high, low), jnp.where(upper, low, high)


def joined(mine, theirs, upper):
    return jnp.where(
        upper,
        jnp.concatenate([theirs, mine], axis=0),
        jnp.concatenate([mine, theirs], axis=0),
    )


def local(rows_n, cols_n, activations, act_basis, out_grads, grad_basis):
    chips = cols_n // CORES
    col = lax.axis_index("col")
    row = lax.axis_index("row")
    core = col & 1
    swap = lambda x: lax.ppermute(x, "col", [(c, c ^ 1) for c in range(cols_n)])
    trade = lambda x, bit: lax.ppermute(x, "row", [(r, r ^ bit) for r in range(rows_n)])
    bits = powers(rows_n)

    succ = chip_ring(chips)
    pred = {b: a for a, b in succ.items()}
    ring = on_both_cores(sorted(succ.items()))
    blocks = [activations]
    pairs = [(activations, swap(activations))]
    grads = copy_gate(out_grads, pairs[0][1])
    pieces = [grads] + [trade(grads, mask) for mask in range(1, rows_n)]
    for bit in bits:
        pieces = [
            joined(low, high, (row & bit) != 0)
            for low, high in zip(pieces[::2], pieces[1::2])
        ]
    grads = pieces[0]
    for s in range(1, chips):
        block = lax.ppermute(blocks[-1], "col", ring)
        if s == 1:
            block = gate(block, grads)
        blocks.append(block)
        pairs.append((block, swap(block)))

    chip_bits = powers(chips)
    chip_trade = lambda x, bit: lax.ppermute(
        x, "col", on_both_cores([(c, c ^ bit) for c in range(chips)])
    )
    upper_chip = (col & CORES) != 0
    plus = lambda a, b: (a.astype(F32) + b.astype(F32)).astype(BF16)

    def plus_others(x, got, others):
        x = plus(x, got)
        for bit in others[1:]:
            x = plus(x, trade(x, bit))
        return x

    half = chips // 2
    width = act_basis.shape[1]
    (start_l, wide_l), (start_r, wide_r) = column_parts(width)
    early = [b for p in pairs[:half] for b in p]
    late = [b for p in pairs[half:] for b in p]

    part = lax.dot_general(
        grad_basis,
        grads,
        (((0,), (1,)), ((), ())),
        preferred_element_type=F32,
    )
    seq_tokens = part.shape[1] // SEQS
    seqs = [part[:, :seq_tokens], part[:, seq_tokens:]]
    mine = jnp.where(core == 0, seqs[0], seqs[1])
    theirs = jnp.where(core == 0, seqs[1], seqs[0]).astype(BF16)
    mine = mine + swap(theirs).astype(F32)
    mine, away = halves(mine, upper_chip)

    early_bit, early_bits = bits[-1], bits[:-1]
    late_bit, late_bits = bits[0], bits[1:]
    early_upper, late_upper = row & early_bit, row & late_bit
    table = []
    for r in range(rows_n):
        for c in range(cols_n):
            here, k = c // CORES, c % CORES
            place = []
            for _ in range(chips):
                block = (here + k * (chips // SEQS)) % chips
                place += [CORES * block + k, CORES * block + 1 - k]
                here = pred[here]
            flat = []
            for at, bit in ((0, early_bit), (chips, late_bit)):
                low, high = place[at : at + half], place[at + half : at + chips]
                flat += high + low if r & bit else low + high
            table.append(flat)
    place = jnp.asarray(np.array(table, np.int32))
    place = lax.dynamic_index_in_dim(place, row * cols_n + col, 0, keepdims=False)

    keep_l, send_l = first_chunk_dot(
        early, act_basis, start_l, wide_l, [theirs, place], early_upper
    )
    got_l = trade(send_l, early_bit)
    keep_r, send_r = chunk_dot(
        early, act_basis, start_r, wide_r, [blocks[half], send_l], early_upper
    )

    keep_l = plus(keep_l, got_l)
    send_r, keep_l, away = gates([send_r, keep_l, away.astype(BF16)])
    got_r = trade(send_r, early_bit)
    got_l = trade(keep_l, early_bits[0])
    got_away = chip_trade(away, 1)
    last = gate(blocks[-1], send_r)
    late[-2:] = [last, swap(last)]
    late_l, send_l = chunk_dot(late, act_basis, start_l, wide_l, [send_r], late_upper)

    got_r, got_l, got_away = gates([got_r, got_l, got_away], send_l)
    mine = mine + got_away.astype(F32)
    early_l = plus_others(keep_l, got_l, early_bits)
    keep_r = plus(keep_r, got_r)
    send_l, early_l, keep_r, away = gates([send_l, early_l, keep_r, mine.astype(BF16)])
    got_l = trade(send_l, late_bit)
    got_r = trade(keep_r, early_bits[0])
    early_other_l = trade(early_l, early_bit)
    for bit in chip_bits[1:]:
        mine = mine + chip_trade(away, bit).astype(F32)
        away = mine.astype(BF16)
    late_r, send_r = chunk_dot(late, act_basis, start_r, wide_r, [send_l], late_upper)

    got_r, got_l = gates([got_r, got_l], send_r, early_other_l)
    early_r = plus_others(keep_r, got_r, early_bits)
    send_r, late_l, early_r = gates([send_r, plus(late_l, got_l), early_r])
    got_r = trade(send_r, late_bit)
    got_l = trade(late_l, late_bits[0])

    late_l = plus_others(late_l, got_l, late_bits)
    late_l, late_r = gates([late_l, plus(late_r, got_r)])
    late_other_l = trade(late_l, late_bit)
    got_r = trade(late_r, late_bits[0])
    other_own = chip_trade(away, 1)

    late_r = plus_others(late_r, got_r, late_bits)
    own = joined(away, other_own, upper_chip)
    late_r, early_r, own = gates([late_r, early_r, own], late_other_l)
    late_other_r = trade(late_r, late_bit)
    early_other_r = trade(early_r, early_bit)
    sib = swap(own)

    unit = activations.shape[0]
    parts_l = [early_l, early_other_l, late_l, late_other_l]
    out = lambda_product(place, own, sib, parts_l, unit, start_l, wide_l, width)
    parts_r = [early_r, early_other_r, late_r, late_other_r]
    return lambda_product(place, own, sib, parts_r, unit, start_r, wide_r, width, out)


def solution(mesh):
    rows_n, cols_n = mesh.shape["row"], mesh.shape["col"]

    def body(activations, act_basis, out_grads, grad_basis):
        return local(rows_n, cols_n, activations, act_basis, out_grads, grad_basis)

    return jax.shard_map(
        body,
        mesh=mesh,
        in_specs=(P("col", "row"), P("row", "col"), P("row", "col"), P("col", "row")),
        out_specs=P("row", "col"),
        check_vma=False,
    )
```

```python
import functools

import jax
import jax.numpy as jnp
import numpy as np
from jax import lax
from jax.experimental import pallas as pl
from jax.experimental.pallas import tpu as pltpu
from jax.sharding import PartitionSpec as P

SEQS = 2
CORES = 2
F32 = jnp.float32
BF16 = jnp.bfloat16
ANYWHERE = pl.BlockSpec(memory_space=pl.ANY)
IN_VMEM = pl.BlockSpec(memory_space=pltpu.VMEM)


def vmem(mib):
    return pltpu.CompilerParams(vmem_limit_bytes=mib * 2**20)


def largest_tile(size, unit, most):
    tile = unit
    for candidate in range(unit, most + 1, unit):
        if size % candidate == 0:
            tile = candidate
    return tile if size % tile == 0 else size


def column_parts(width):
    right = width // 2 if width % 512 == 0 else 128
    return [(0, width - right), (width - right, right)]


def column_tile(start, width, most=256):
    for tile in (512, 256, 128):
        if tile <= most and start % tile == 0 and width % tile == 0:
            return tile
    raise ValueError("columns")


NO_COST = pl.CostEstimate(flops=0, bytes_accessed=0, transcendentals=0)


def gates(arrays, *after):
    count = len(arrays)
    return pl.pallas_call(
        lambda *refs: None,
        in_specs=[ANYWHERE] * (count + len(after)),
        out_specs=[ANYWHERE] * count,
        out_shape=[jax.ShapeDtypeStruct(x.shape, x.dtype) for x in arrays],
        input_output_aliases={i: i for i in range(count)},
        compiler_params=vmem(1),
        cost_estimate=NO_COST,
        name="gates",
    )(*arrays, *after)


def gate(x, *after):
    return gates([x], *after)[0]


def copy_gate(x, after):
    def kernel(x_ref, after_ref, out_ref):
        out_ref[...] = x_ref[...]

    return pl.pallas_call(
        kernel,
        in_specs=[pl.BlockSpec(memory_space=pltpu.VMEM), ANYWHERE],
        out_specs=pl.BlockSpec(memory_space=pltpu.VMEM),
        out_shape=jax.ShapeDtypeStruct(x.shape, x.dtype),
        compiler_params=vmem(2),
        cost_estimate=NO_COST,
        name="copy_gate",
    )(x, after)


def chunk_dot(blocks, basis, start, width, after, upper):
    rows, depth = blocks[0].shape
    tokens = rows * len(blocks)
    tile = column_tile(start, width)
    first = start // tile
    deep = depth // 2
    count = len(blocks)

    def kernel(upper_ref, *rest):
        block_refs, top_ref, low_ref = rest[:count], rest[count], rest[count + 1]
        keep_ref, send_ref, joint = rest[-3:]

        @pl.when(pl.program_id(0) == 0)
        def _():
            for i, block_ref in enumerate(block_refs):
                joint[i * rows : (i + 1) * rows, :] = block_ref[...]

        total = jnp.dot(joint[:, :deep], top_ref[...], preferred_element_type=F32)
        total += jnp.dot(joint[:, deep:], low_ref[...], preferred_element_type=F32)
        total = total.astype(BF16)
        half = tokens // 2
        is_upper = upper_ref[0] != 0
        keep_ref[...] = jnp.where(is_upper, total[half:], total[:half])
        send_ref[...] = jnp.where(is_upper, total[:half], total[half:])

    out_rows = tokens // 2
    return pl.pallas_call(
        kernel,
        grid_spec=pltpu.PrefetchScalarGridSpec(
            num_scalar_prefetch=1,
            grid=(width // tile,),
            in_specs=[IN_VMEM] * count
            + [
                pl.BlockSpec((deep, tile), lambda n, s: (0, first + n)),
                pl.BlockSpec((deep, tile), lambda n, s: (1, first + n)),
            ]
            + [ANYWHERE] * len(after),
            out_specs=[pl.BlockSpec((out_rows, tile), lambda n, s: (0, n))] * 2,
            scratch_shapes=[pltpu.VMEM((tokens, depth), BF16)],
        ),
        out_shape=[jax.ShapeDtypeStruct((out_rows, width), BF16)] * 2,
        compiler_params=vmem(14),
        cost_estimate=pl.CostEstimate(
            flops=2 * tokens * depth * width,
            bytes_accessed=2 * depth * width,
            transcendentals=0,
        ),
        name="chunk_dot",
    )(jnp.reshape(upper, (1,)), *blocks, basis, basis, *after)


def first_chunk_dot(blocks, basis, start, width, after, upper):
    part = jnp.dot(
        gate(jnp.concatenate(blocks, axis=0), *after),
        basis[:, start : start + width],
        preferred_element_type=F32,
    )
    return halves(part.astype(BF16), upper != 0)


def lambda_product(place, own, sib, parts, unit, start, width, whole, so_far=None):
    out_rows, seq_tokens = own.shape
    tile_o = largest_tile(out_rows, 128, 256)
    tile_n = min(512, width)
    at_block = start // width
    count = len(parts)
    given = [] if so_far is None else [so_far]

    def kernel(place_ref, own_ref, sib_ref, *rest):
        part_refs, out_ref, acts = rest[:count], rest[-2], rest[-1]

        @pl.when(pl.program_id(0) == 0)
        def _():
            at = 0
            for part in part_refs:
                for h in range(part.shape[0] // unit):
                    rows = pl.ds(pl.multiple_of(place_ref[at] * unit, unit), unit)
                    acts[rows, :] = part[h * unit : (h + 1) * unit, :]
                    at += 1

        for n in range(0, width, tile_n):
            cols = pl.ds(n, min(tile_n, width - n))
            first = jnp.dot(own_ref[...], acts[:seq_tokens, cols], preferred_element_type=F32)
            second = jnp.dot(sib_ref[...], acts[seq_tokens:, cols], preferred_element_type=F32)
            mean = (first * first + second * second) * (1.0 / SEQS)
            out_ref[:, cols] = mean.astype(BF16)

    return pl.pallas_call(
        kernel,
        grid_spec=pltpu.PrefetchScalarGridSpec(
            num_scalar_prefetch=1,
            grid=(out_rows // tile_o,),
            in_specs=[pl.BlockSpec((tile_o, seq_tokens), lambda o, s: (o, 0))] * 2
            + [IN_VMEM] * count
            + [ANYWHERE] * len(given),
            out_specs=pl.BlockSpec((tile_o, width), lambda o, s: (o, at_block)),
            scratch_shapes=[pltpu.VMEM((SEQS * seq_tokens, width), BF16)],
        ),
        out_shape=jax.ShapeDtypeStruct((out_rows, whole), BF16),
        input_output_aliases={3 + count: 0} if given else {},
        compiler_params=vmem(8),
        cost_estimate=pl.CostEstimate(
            flops=2 * out_rows * width * SEQS * seq_tokens,
            bytes_accessed=2 * out_rows * width,
            transcendentals=0,
        ),
        name="lambda_product",
    )(place, own, sib, *parts, *given)


def chip_ring(chips):
    order = list(range(1, chips, 2))
    order = [0] + order + [c for c in range(chips - 1, 0, -1) if c % 2 == 0]
    return {order[i]: order[(i + 1) % chips] for i in range(chips)}


def on_both_cores(pairs):
    return [(CORES * a + k, CORES * b + k) for a, b in pairs for k in range(CORES)]


def powers(n):
    return [1 << b for b in range(n.bit_length() - 1)]


def halves(x, upper):
    half = x.shape[0] // 2
    low, high = x[:half], x[half:]
    return jnp.where(upper, high, low), jnp.where(upper, low, high)


def joined(mine, theirs, upper):
    return jnp.where(
        upper,
        jnp.concatenate([theirs, mine], axis=0),
        jnp.concatenate([mine, theirs], axis=0),
    )


def local(rows_n, cols_n, activations, act_basis, out_grads, grad_basis):
    chips = cols_n // CORES
    col = lax.axis_index("col")
    row = lax.axis_index("row")
    core = col & 1
    swap = lambda x: lax.ppermute(x, "col", [(c, c ^ 1) for c in range(cols_n)])
    trade = lambda x, bit: lax.ppermute(x, "row", [(r, r ^ bit) for r in range(rows_n)])
    bits = powers(rows_n)

    succ = chip_ring(chips)
    pred = {b: a for a, b in succ.items()}
    ring = on_both_cores(sorted(succ.items()))
    blocks = [activations]
    pairs = [(activations, swap(activations))]
    grads = copy_gate(out_grads, pairs[0][1])
    pieces = [grads] + [trade(grads, mask) for mask in range(1, rows_n)]
    for bit in bits:
        pieces = [
            joined(low, high, (row & bit) != 0)
            for low, high in zip(pieces[::2], pieces[1::2])
        ]
    grads = pieces[0]
    for s in range(1, chips):
        block = lax.ppermute(blocks[-1], "col", ring)
        if s == 1:
            block = gate(block, grads)
        blocks.append(block)
        pairs.append((block, swap(block)))

    chip_bits = powers(chips)
    chip_trade = lambda x, bit: lax.ppermute(
        x, "col", on_both_cores([(c, c ^ bit) for c in range(chips)])
    )
    upper_chip = (col & CORES) != 0
    plus = lambda a, b: (a.astype(F32) + b.astype(F32)).astype(BF16)

    def plus_others(x, got, others):
        x = plus(x, got)
        for bit in others[1:]:
            x = plus(x, trade(x, bit))
        return x

    half = chips // 2
    width = act_basis.shape[1]
    (start_l, wide_l), (start_r, wide_r) = column_parts(width)
    early = [b for p in pairs[:half] for b in p]
    late = [b for p in pairs[half:] for b in p]

    part = lax.dot_general(
        grad_basis,
        grads,
        (((0,), (1,)), ((), ())),
        preferred_element_type=F32,
    )
    seq_tokens = part.shape[1] // SEQS
    seqs = [part[:, :seq_tokens], part[:, seq_tokens:]]
    mine = jnp.where(core == 0, seqs[0], seqs[1])
    theirs = jnp.where(core == 0, seqs[1], seqs[0]).astype(BF16)
    mine = mine + swap(theirs).astype(F32)
    mine, away = halves(mine, upper_chip)

    early_bit, early_bits = bits[-1], bits[:-1]
    late_bit, late_bits = bits[0], bits[1:]
    early_upper, late_upper = row & early_bit, row & late_bit
    table = []
    for r in range(rows_n):
        for c in range(cols_n):
            here, k = c // CORES, c % CORES
            place = []
            for _ in range(chips):
                block = (here + k * (chips // SEQS)) % chips
                place += [CORES * block + k, CORES * block + 1 - k]
                here = pred[here]
            flat = []
            for at, bit in ((0, early_bit), (chips, late_bit)):
                low, high = place[at : at + half], place[at + half : at + chips]
                flat += high + low if r & bit else low + high
            table.append(flat)
    place = jnp.asarray(np.array(table, np.int32))
    place = lax.dynamic_index_in_dim(place, row * cols_n + col, 0, keepdims=False)

    keep_l, send_l = first_chunk_dot(
        early, act_basis, start_l, wide_l, [theirs, place], early_upper
    )
    got_l = trade(send_l, early_bit)
    keep_r, send_r = chunk_dot(
        early, act_basis, start_r, wide_r, [blocks[half], send_l], early_upper
    )

    keep_l = plus(keep_l, got_l)
    send_r, keep_l, away = gates([send_r, keep_l, away.astype(BF16)])
    got_r = trade(send_r, early_bit)
    got_l = trade(keep_l, early_bits[0])
    got_away = chip_trade(away, 1)
    last = gate(blocks[-1], send_r)
    late[-2:] = [last, swap(last)]
    late_l, send_l = chunk_dot(late, act_basis, start_l, wide_l, [send_r], late_upper)

    got_r, got_l, got_away = gates([got_r, got_l, got_away], send_l)
    mine = mine + got_away.astype(F32)
    early_l = plus_others(keep_l, got_l, early_bits)
    keep_r = plus(keep_r, got_r)
    send_l, early_l, keep_r, away = gates([send_l, early_l, keep_r, mine.astype(BF16)])
    got_l = trade(send_l, late_bit)
    got_r = trade(keep_r, early_bits[0])
    early_other_l = trade(early_l, early_bit)
    for bit in chip_bits[1:]:
        mine = mine + chip_trade(away, bit).astype(F32)
        away = mine.astype(BF16)
    late_r, send_r = chunk_dot(late, act_basis, start_r, wide_r, [send_l], late_upper)

    got_r, got_l = gates([got_r, got_l], send_r, early_other_l)
    early_r = plus_others(keep_r, got_r, early_bits)
    send_r, late_l, early_r = gates([send_r, plus(late_l, got_l), early_r])
    got_r = trade(send_r, late_bit)
    got_l = trade(late_l, late_bits[0])

    late_l = plus_others(late_l, got_l, late_bits)
    late_l, late_r = gates([late_l, plus(late_r, got_r)])
    late_other_l = trade(late_l, late_bit)
    got_r = trade(late_r, late_bits[0])
    other_own = chip_trade(away, 1)

    late_r = plus_others(late_r, got_r, late_bits)
    own = joined(away, other_own, upper_chip)
    late_r, early_r, own = gates([late_r, early_r, own], late_other_l)
    late_other_r = trade(late_r, late_bit)
    early_other_r = trade(early_r, early_bit)
    sib = swap(own)

    unit = activations.shape[0]
    parts_l = [early_l, early_other_l, late_l, late_other_l]
    out = lambda_product(place, own, sib, parts_l, unit, start_l, wide_l, width)
    parts_r = [early_r, early_other_r, late_r, late_other_r]
    return lambda_product(place, own, sib, parts_r, unit, start_r, wide_r, width, out)


def solution(mesh):
    rows_n, cols_n = mesh.shape["row"], mesh.shape["col"]

    def body(activations, act_basis, out_grads, grad_basis):
        return local(rows_n, cols_n, activations, act_basis, out_grads, grad_basis)

    return jax.shard_map(
        body,
        mesh=mesh,
        in_specs=(P("col", "row"), P("row", "col"), P("row", "col"), P("col", "row")),
        out_specs=P("row", "col"),
        check_vma=False,
    )
```
